32 devices in a mesh: dp: 8 (over z, x), seq: 4 (over y, core).
Axes of the slice: x: 2, y: 2, z: 4, core: 2. Of those that a mesh axis runs over, the one named last changes fastest.
Arguments:
- tokens: bfloat16 [8, 1024, 2048], P('dp', 'seq'), may hold values from -6 to 6
- segments: int32 [8, 1024], P('dp'), may hold values from 0 to 2, as said below
- positions: int32 [8, 1024], P('dp'), may hold values from 0 to 1023, as said below
- ln1_gain: bfloat16 [2048], P(('dp', 'seq')), may hold values from 0.25 to 1.75
- ln1_bias: bfloat16 [2048], P(('dp', 'seq')), may hold values from -1 to 1
- ln2_gain: bfloat16 [2048], P(('dp', 'seq')), may hold values from 0.25 to 1.75
- ln2_bias: bfloat16 [2048], P(('dp', 'seq')), may hold values from -1 to 1
- qkv_weight: bfloat16 [2048, 6144], P(('dp', 'seq')), may hold values from -0.125 to 0.125
- qkv_bias: bfloat16 [6144], P(('dp', 'seq')), may hold values from -1 to 1
- dense_weight: bfloat16 [2048, 2048], P(('dp', 'seq')), may hold values from -1 to 1
- dense_bias: bfloat16 [2048], P(('dp', 'seq')), may hold values from -1 to 1
- fc1_weight: bfloat16 [2048, 8192], P(('dp', 'seq')), may hold values from -0.125 to 0.125
- fc1_bias: bfloat16 [8192], P(('dp', 'seq')), may hold values from -1 to 1
- fc2_weight: bfloat16 [8192, 2048], P(('dp', 'seq')), may hold values from -0.0625 to 0.0625
- fc2_bias: bfloat16 [2048], P(('dp', 'seq')), may hold values from -1 to 1
- cotangent: bfloat16 [8, 1024, 2048], P('dp', 'seq'), may hold values from -6 to 6
Outputs:
- output: bfloat16 [8, 1024, 2048], P('dp', 'seq')
- grad_tokens: float32 [8, 1024, 2048], P('dp', 'seq')
- grad_ln1_gain: float32 [2048], P(('dp', 'seq'))
- grad_ln1_bias: float32 [2048], P(('dp', 'seq'))
- grad_ln2_gain: float32 [2048], P(('dp', 'seq'))
- grad_ln2_bias: float32 [2048], P(('dp', 'seq'))
- grad_qkv_weight: float32 [2048, 6144], P(('dp', 'seq'))
- grad_qkv_bias: float32 [6144], P(('dp', 'seq'))
- grad_dense_weight: float32 [2048, 2048], P(('dp', 'seq'))
- grad_dense_bias: float32 [2048], P(('dp', 'seq'))
- grad_fc1_weight: float32 [2048, 8192], P(('dp', 'seq'))
- grad_fc1_bias: float32 [8192], P(('dp', 'seq'))
- grad_fc2_weight: float32 [8192, 2048], P(('dp', 'seq'))
- grad_fc2_bias: float32 [2048], P(('dp', 'seq'))
The draws below stay inside these ranges and needn't reach their ends.
Inputs may be any that keep to these rules, and one draw needn't show every extreme that they name: `segments`: in each sequence the ids are 0 before a first cut, 1 from it up to a second cut and 2 from there on; the first cut lies among positions 1 to 255 and the second among the last 255 positions. Within segments 1 and 2 a token's position is its distance from its segment's first token; in segment 0 positions rise by one along the sequence and its last token has position 1023.
All inputs are finite; a program needn't handle non-finite values.
Results may differ from the reference program's by a relative error of at most 0.0089.
Values may be sent and summed in bfloat16 or wider, within the bound.
No kernel may reach another device: no remote copies, remote signals or barrier semaphores. Data moves between devices by JAX's collectives and lax.ppermute only.
A program may use at most 448 MiB of HBM per device.

```python
import math
import jax
import jax.numpy as jnp
from jax import lax

D = 2048
HEADS = 8
ROT_DIMS = 64
FF = 8192
POS_DEV = 256
BATCH = 8
SEQ_LEN = 1024


def document_cuts(key):
    first_key, last_key = jax.random.split(key, 2)
    first_cut = jax.random.randint(first_key, (BATCH, 1), 1, POS_DEV)
    second_cut = jax.random.randint(last_key, (BATCH, 1), SEQ_LEN - POS_DEV + 1, SEQ_LEN)
    index = jnp.arange(SEQ_LEN, dtype=jnp.int32)[None, :]
    return (first_cut, second_cut, index)


def draw_segments(key, part):
    first_cut, second_cut, index = document_cuts(key)
    seg_ids = (index >= first_cut).astype(jnp.int32) + (index >= second_cut).astype(jnp.int32)
    return seg_ids.astype(jnp.int32)


def draw_positions(key, part):
    first_cut, second_cut, index = document_cuts(key)
    inside = jnp.where(index < second_cut, index - first_cut, index - second_cut)
    leading = index + (SEQ_LEN - first_cut)
    pos_ids = jnp.where(index < first_cut, leading, inside)
    return pos_ids.astype(jnp.int32)


def spiked(values, own_key, source, target, shards_of, factor):
    def block_of(axis_at):
        return (jnp.arange(values.shape[axis_at]) // (values.shape[axis_at] // shards_of)).reshape((-1,) + (1,) * (values.ndim - 1 - axis_at))

    near = jax.random.permutation(own_key, shards_of)[block_of(target)]
    other_side = (block_of(target) + shards_of // 2) % shards_of
    return jnp.where((block_of(source) == near) | (block_of(source) == other_side), factor * values, values)


def block_scale(key, extent, shards, low, top_value):
    level = 1.0
    for dim, blocks in shards:
        draws = jax.random.uniform(jax.random.fold_in(jax.random.fold_in(key, 6), dim), (blocks,), jnp.float32, low / len(shards), top_value / len(shards))
        level = level * jnp.repeat(jnp.exp(draws), extent[dim] // blocks).reshape((-1,) + (1,) * (len(extent) - 1 - dim))
    return level


def gaussian(stream_key, dims, scale, limit, cuts=(), kind=jnp.bfloat16):
    gain = block_scale(stream_key, dims, cuts, -0.22, 0.18) if cuts else 1.0
    values = jax.random.normal(stream_key, dims, jnp.float32) * scale * gain
    return jnp.minimum(jnp.maximum(values, -limit), limit).astype(kind)


def heavy_noise(stream_key, extent, scale, bound, cuts, heavy, held_as=jnp.bfloat16):
    values = scale * jax.random.normal(stream_key, extent, jnp.float32)
    if cuts:
        values = values * block_scale(stream_key, extent, cuts, -0.22, 0.18)
    return jnp.clip(spiked(values, jax.random.fold_in(stream_key, 3), *heavy), -bound, bound).astype(held_as)


def setup_inputs(seed: int = 0) -> dict:
    streams_of = jax.random.split(jax.random.key(seed), 17)
    tokens = gaussian(streams_of[0], (BATCH, SEQ_LEN, D), 1.0, 6.0, ((0, 8), (1, 4)))
    segments = draw_segments(jax.random.fold_in(streams_of[16], 71), 0)
    positions = draw_positions(jax.random.fold_in(streams_of[16], 71), 0)
    ln1_gain = jnp.clip(1.0 + 0.15 * jax.random.normal(streams_of[3], (D,), jnp.float32), 0.25, 1.75).astype(jnp.bfloat16)
    ln1_bias = gaussian(streams_of[4], (D,), 0.2, 1.0, ((0, 32),))
    ln2_gain = jnp.clip(1.0 + 0.15 * jax.random.normal(streams_of[5], (D,), jnp.float32), 0.25, 1.75).astype(jnp.bfloat16)
    ln2_bias = gaussian(streams_of[6], (D,), 0.2, 1.0, ((0, 32),))
    qkv_weight = gaussian(streams_of[7], (D, 3 * D), D ** -0.5, 0.125, ((0, 32),))
    qkv_bias = gaussian(streams_of[8], (3 * D,), 0.2, 1.0, ((0, 32),))
    dense_weight = gaussian(streams_of[9], (D, D), (D // 64) ** -0.5, 1.0, ((0, 32),))
    dense_bias = gaussian(streams_of[10], (D,), 0.2, 1.0, ((0, 32),))
    fc1_weight = gaussian(streams_of[11], (D, FF), D ** -0.5, 0.125, ((0, 32),))
    fc1_bias = gaussian(streams_of[12], (FF,), 0.2, 1.0, ((0, 32),))
    fc2_weight = gaussian(streams_of[13], (FF, D), FF ** -0.5, 0.0625, ((0, 32),))
    fc2_bias = gaussian(streams_of[14], (D,), 0.2, 1.0, ((0, 32),))
    cotangent = heavy_noise(streams_of[15], (BATCH, SEQ_LEN, D), 1.0, 6.0, ((0, 8), (1, 4)), (0, 2, 8, 2.0))
    return {"tokens": tokens, "segments": segments, "positions": positions, "ln1_gain": ln1_gain, "ln1_bias": ln1_bias, "ln2_gain": ln2_gain, "ln2_bias": ln2_bias, "qkv_weight": qkv_weight, "qkv_bias": qkv_bias, "dense_weight": dense_weight, "dense_bias": dense_bias, "fc1_weight": fc1_weight, "fc1_bias": fc1_bias, "fc2_weight": fc2_weight, "fc2_bias": fc2_bias, "cotangent": cotangent}


@jax.custom_vjp
def low(v):
    return lax.optimization_barrier(v.astype(jnp.bfloat16)).astype(jnp.float32)

@jax.custom_vjp
def low_back(v):
    return v

def low_keep(v):
    return (low(v), None)

def low_pass(kept, grad):
    return (grad,)

def back_keep(v):
    return (v, None)

def back_low(kept, grad):
    return (low(grad),)
low.defvjp(low_keep, low_pass)
low_back.defvjp(back_keep, back_low)
highest = lax.Precision.HIGHEST
root_half = 0.7071067811865476

def normalize(values):
    average = lax.optimization_barrier(jnp.mean(values, axis=-1, keepdims=True))
    centred = values - average
    inv_std = lax.rsqrt(lax.optimization_barrier(jnp.mean(centred * centred, axis=-1, keepdims=True)) + 1e-05)
    return (centred * inv_std, inv_std)

def rotary_tables(positions, rot_dims):
    halfway = rot_dims // 2
    inverse = 10000.0 ** (-(2.0 * jnp.arange(halfway, dtype=jnp.float32)) / rot_dims)
    angles = positions.astype(jnp.float32)[..., None] * inverse
    return (jnp.cos(angles), jnp.sin(angles))

def rotate(vectors, cosines, sines, rot_dims):
    halfway = rot_dims // 2
    first_half = vectors[..., :halfway]
    second_half = vectors[..., halfway:rot_dims]
    cos_wide = cosines[..., None, :]
    sin_wide = sines[..., None, :]
    return jnp.concatenate([first_half * cos_wide - second_half * sin_wide, second_half * cos_wide + first_half * sin_wide, vectors[..., rot_dims:]], axis=-1)

def block(inputs, seg_ids, pos_ids, weights):
    gain_one, shift_one, gain_two, shift_two, w_qkv, b_qkv, w_dense, b_dense, w_up, b_up, w_down, b_down = weights
    group, seq_len, width = inputs.shape
    head_dim = width // HEADS
    factor = head_dim ** (-0.5)
    normed_x, inv_std = normalize(inputs)
    normed_one = low(normed_x * gain_one + shift_one)
    normed_two = low(normed_x * gain_two + shift_two)
    projected = low_back(jnp.einsum('gld,de->gle', normed_one, w_qkv, precision=highest) + b_qkv)
    projected = projected.reshape(group, seq_len, HEADS, 3, head_dim)
    cosines, sines = rotary_tables(pos_ids, ROT_DIMS)
    queries = low(rotate(projected[:, :, :, 0], cosines, sines, ROT_DIMS))
    keys = low(rotate(projected[:, :, :, 1], cosines, sines, ROT_DIMS))
    values = low(projected[:, :, :, 2])
    raw_scores = low_back(jnp.einsum('gqhd,gkhd->ghqk', queries, keys, precision=highest) * factor)
    index = jnp.arange(seq_len, dtype=jnp.int32)
    allowed = (seg_ids[:, :, None] == seg_ids[:, None, :]) & (index[None, None, :] <= index[None, :, None])
    masked = jnp.where(allowed[:, None], raw_scores, -1e+30)
    largest = lax.optimization_barrier(jnp.max(masked, axis=-1, keepdims=True))
    expo = jnp.exp(masked - largest)
    attn_probs = expo / lax.optimization_barrier(jnp.sum(expo, axis=-1, keepdims=True))
    attended = jnp.einsum('ghqk,gkhd->gqhd', low(attn_probs), values, precision=highest)
    attended = low(low_back(attended)).reshape(group, seq_len, width)
    attn_out = jnp.einsum('gld,de->gle', attended, w_dense, precision=highest) + b_dense
    hidden_pre = low_back(jnp.einsum('gld,df->glf', normed_two, w_up, precision=highest) + b_up)
    activated = low(hidden_pre * 0.5 * (1.0 + jax.scipy.special.erf(hidden_pre * root_half)))
    mlp_out = jnp.einsum('glf,fd->gld', activated, w_down, precision=highest) + b_down
    return inputs + attn_out + mlp_out

def reference(tokens, segments, positions, ln1_gain, ln1_bias, ln2_gain, ln2_bias, qkv_weight, qkv_bias, dense_weight, dense_bias, fc1_weight, fc1_bias, fc2_weight, fc2_bias, cotangent):
    params = (ln1_gain.astype(jnp.float32), ln1_bias.astype(jnp.float32), ln2_gain.astype(jnp.float32), ln2_bias.astype(jnp.float32), qkv_weight.astype(jnp.float32), qkv_bias.astype(jnp.float32), dense_weight.astype(jnp.float32), dense_bias.astype(jnp.float32), fc1_weight.astype(jnp.float32), fc1_bias.astype(jnp.float32), fc2_weight.astype(jnp.float32), fc2_bias.astype(jnp.float32))
    group = math.gcd(BATCH, max(1, 4096 // SEQ_LEN))
    rounds = BATCH // group

    def grouped(array):
        return array.reshape((rounds, group) + array.shape[1:])
    items = (grouped(tokens.astype(jnp.float32)), grouped(segments), grouped(positions), grouped(cotangent.astype(jnp.float32)))

    def one_round(totals, item):
        inputs, seg_ids, pos_ids, upstream = item

        def forward(values, weights):
            return block(values, seg_ids, pos_ids, weights)
        result, pullback = jax.vjp(forward, inputs, params)
        grad_inputs, grad_params = pullback(upstream)
        updated = tuple((total + extra for total, extra in zip(totals, grad_params)))
        return (updated, (result.astype(jnp.bfloat16), grad_inputs))
    zeros = tuple((jnp.zeros(p.shape, jnp.float32) for p in params))
    totals, (results, grads_in) = lax.scan(one_round, zeros, items)
    output = results.reshape(tokens.shape)
    grad_tokens = grads_in.reshape(tokens.shape)
    return (output, grad_tokens, totals[0], totals[1], totals[2], totals[3], totals[4], totals[5], totals[6], totals[7], totals[8], totals[9], totals[10], totals[11])
```

```python
import jax
import jax.numpy as jnp
from jax import lax
from jax.sharding import PartitionSpec as P

HEADS = 8
ROT_DIMS = 64
AXES = ("dp", "seq")

root_half = 0.7071067811865476
inv_root_tau = 0.3989422804014327
bf16 = jnp.bfloat16
f32 = jnp.float32


def normalize(values):
    average = jnp.mean(values, axis=-1, keepdims=True)
    centred = values - average
    inv_std = lax.rsqrt(jnp.mean(centred * centred, axis=-1, keepdims=True) + 1e-05)
    return (centred * inv_std, inv_std)


def rotary_tables(positions, rot_dims):
    halfway = rot_dims // 2
    inverse = 10000.0 ** (-(2.0 * jnp.arange(halfway, dtype=f32)) / rot_dims)
    angles = positions[..., None] * inverse
    return (jnp.cos(angles), jnp.sin(angles))


def rotate(vectors, cosines, sines, rot_dims):
    halfway = rot_dims // 2
    first_half = vectors[..., :halfway]
    second_half = vectors[..., halfway:rot_dims]
    return jnp.concatenate(
        [
            first_half * cosines - second_half * sines,
            second_half * cosines + first_half * sines,
            vectors[..., rot_dims:],
        ],
        axis=-1,
    )


def column_products(matrix, second_matrix):
    return lax.dot_general(
        matrix, second_matrix, (((0,), (0,)), ((), ())), preferred_element_type=f32
    )


def times_back(matrix, second_matrix):
    return lax.dot_general(
        matrix, second_matrix, (((1,), (1,)), ((), ())), preferred_element_type=f32
    )


def times(matrix, second_matrix):
    return jnp.dot(matrix, second_matrix, preferred_element_type=f32)


def pick(array, index):
    return lax.dynamic_index_in_dim(array, index, 0, keepdims=False)


def put(array, value, index):
    return lax.dynamic_update_index_in_dim(array, value, index, 0)


class Block:
    def __init__(self, total):
        self.blocks = total // 8
        self.total = total
        index = lax.axis_index(AXES)
        self.r = index // 8
        self.g = index % 8
        self.pq = self.g // 2
        self.c = self.g % 2

    def swap(self, array, mask):
        return lax.ppermute(array, AXES, [(i, i ^ mask) for i in range(self.total)])

    def along(self, array, step, low, high):
        pairs = [
            (8 * r + g, 8 * ((r + step) % self.blocks) + g)
            for r in range(low, high)
            for g in range(8)
        ]
        return lax.ppermute(array, AXES, pairs)

    def gather_core(self, array):
        other = self.swap(array, 1)
        out = jnp.zeros((2,) + array.shape, array.dtype)
        return put(put(out, array, self.c), other, 1 - self.c)

    def gather_square(self, array):
        half = array.shape[0] // 2
        one, two = array[:half], array[half:]
        one_p, two_q = self.swap(one, 4), self.swap(two, 2)
        one_q, two_p = (
            self.swap(jnp.stack([one, one_p]), 2),
            self.swap(jnp.stack([two, two_q]), 4),
        )
        first = jnp.zeros((4,) + one.shape, array.dtype)
        second = jnp.zeros((4,) + two.shape, array.dtype)
        for value, mask in ((one, 0), (one_p, 2), (one_q[0], 1), (one_q[1], 3)):
            first = put(first, value, self.pq ^ mask)
        for value, mask in ((two, 0), (two_q, 1), (two_p[0], 2), (two_p[1], 3)):
            second = put(second, value, self.pq ^ mask)
        return jnp.concatenate([first, second], axis=1)

    def gather_block(self, array):
        square = self.gather_square(array)
        both = self.gather_core(square)
        return jnp.swapaxes(both, 0, 1).reshape((8,) + array.shape)

    def scatter_block(self, parts):
        parts = parts.reshape((4, 2) + parts.shape[1:])
        parts = jnp.swapaxes(parts, 0, 1)
        sent = self.swap(pick(parts, 1 - self.c), 1)
        square = pick(parts, self.c).astype(f32) + sent.astype(f32)
        half = square.shape[1] // 2
        one = square[:, :half].astype(bf16)
        two = square[:, half:].astype(bf16)
        p, q = self.pq // 2, self.pq % 2
        one = one.reshape((2, 2) + one.shape[1:])
        two = jnp.swapaxes(two.reshape((2, 2) + two.shape[1:]), 0, 1)
        one_sent, two_sent = self.swap(pick(one, 1 - p), 4), self.swap(pick(two, 1 - q), 2)
        one = pick(one, p).astype(f32) + one_sent.astype(f32)
        two = pick(two, q).astype(f32) + two_sent.astype(f32)
        one_sent = self.swap(pick(one, 1 - q).astype(bf16), 2)
        two_sent = self.swap(pick(two, 1 - p).astype(bf16), 4)
        return jnp.concatenate(
            [pick(one, q) + one_sent.astype(f32), pick(two, p) + two_sent.astype(f32)]
        )

    def exchange(self, parts):
        parts = parts.reshape((4, 2) + parts.shape[1:])
        parts = jnp.swapaxes(parts, 0, 1)
        sent = self.swap(pick(parts, 1 - self.c), 1)
        both = jnp.zeros_like(parts)
        both = put(put(both, pick(parts, self.c), self.c), sent, 1 - self.c)
        both = jnp.swapaxes(both, 0, 1)
        out = put(jnp.zeros_like(both), pick(both, self.pq), self.pq)
        for mask in (1, 2, 3):
            out = put(out, self.swap(pick(both, self.pq ^ mask), 2 * mask), self.pq ^ mask)
        return out.reshape((8,) + parts.shape[2:])

    def gather_blocks(self, array):
        count = self.blocks
        up, down = [array], [array]
        for step in range(1, count):
            up.append(self.along(up[-1], 1, step - 1, count - 1))
            down.append(self.along(down[-1], -1, 1, count - step + 1))
        out = put(jnp.zeros((count,) + array.shape, array.dtype), array, self.r)
        for step in range(1, count):
            value = jnp.where(self.r >= step, up[step], down[count - step])
            out = put(out, value, (self.r - step) % count)
        return out

    def scatter_blocks(self, parts):
        count = self.blocks
        up = down = None
        for step in range(count - 1, 0, -1):
            above = pick(parts, jnp.minimum(self.r + step, count - 1))
            below = pick(parts, jnp.maximum(self.r - step, 0))
            if up is not None:
                above = (above.astype(f32) + up.astype(f32)).astype(bf16)
                below = (below.astype(f32) + down.astype(f32)).astype(bf16)
            up = self.along(above, 1, 0, count - step)
            down = self.along(below, -1, step, count)
        return pick(parts, self.r).astype(f32) + up.astype(f32) + down.astype(f32)

    def to_heads(self, array, back=False):
        pairs = [(h * self.blocks + r, r * 8 + h) for h in range(8) for r in range(self.blocks)]
        if back:
            pairs = [(b, a) for a, b in pairs]
        return lax.ppermute(array, AXES, pairs)

    def gather_small(self, array):
        count = self.blocks
        out = put(jnp.zeros((count,) + array.shape, array.dtype), array, self.r)
        for step in range(1, count):
            out = put(out, self.along(array, step, 0, count), (self.r - step) % count)
        every = jnp.zeros((4,) + out.shape, array.dtype)
        every = put(every, out, self.pq)
        for mask in (1, 2, 3):
            every = put(every, self.swap(out, 2 * mask), self.pq ^ mask)
        both = self.gather_core(every)
        both = jnp.moveaxis(both, 2, 0)
        return jnp.swapaxes(both, 1, 2).reshape((self.total,) + array.shape)

    def scatter_small(self, block_parts, own_parts):
        count = self.blocks
        parts = block_parts.reshape(count, 2, 2, 2, -1)
        parts = jnp.moveaxis(parts, 0, 3)
        for axis, mask, bit in ((0, 4, self.pq // 2), (0, 2, self.pq % 2), (0, 1, self.c)):
            sent = self.swap(pick(parts, 1 - bit), mask)
            parts = pick(parts, bit) + sent
        parts = jnp.concatenate([parts, own_parts], axis=-1)
        total = pick(parts, self.r)
        for step in range(1, count):
            total = total + self.along(pick(parts, (self.r + step) % count), step, 0, count)
        return total


def on_device(
    tokens,
    segments,
    positions,
    ln1_gain,
    ln1_bias,
    ln2_gain,
    ln2_bias,
    qkv_weight,
    qkv_bias,
    dense_weight,
    dense_bias,
    fc1_weight,
    fc1_bias,
    fc2_weight,
    fc2_bias,
    cotangent,
):
    total = lax.axis_size("dp") * lax.axis_size("seq")
    block = Block(total)
    count = block.blocks
    num_seqs, pos_dev, width = tokens.shape
    seq_len = segments.shape[1]
    rows = num_seqs * pos_dev
    group_rows = 8 * rows
    head_dim = width // HEADS
    factor = head_dim ** (-0.5)
    near = qkv_weight.shape[0]
    units = fc2_weight.shape[0]
    own_tokens = tokens.reshape(rows, width)
    own_up = cotangent.reshape(rows, width)

    small = jnp.concatenate(
        [ln1_gain, ln1_bias, ln2_gain, ln2_bias, dense_bias + 0, fc2_bias, qkv_bias, fc1_bias]
    )
    small = block.gather_small(small)
    sizes = [near] * 6 + [qkv_bias.shape[0], units]
    starts = [sum(sizes[:k]) for k in range(len(sizes) + 1)]
    gain_one, shift_one, gain_two, shift_two, b_dense, b_down, b_qkv, b_up = (
        small[:, starts[k] : starts[k + 1]].reshape(-1).astype(f32) for k in range(8)
    )
    b_qkv = pick(b_qkv.reshape(8, 3 * head_dim), block.g)
    b_up = lax.dynamic_index_in_dim(
        b_up.reshape(count, 8, units), block.g, 1, keepdims=False
    ).reshape(-1)
    places = jnp.concatenate([positions, segments]).astype(f32)[None]
    far = block.swap(places, 4)
    first = block.pq // 2 == 0
    places = jnp.concatenate([jnp.where(first, places, far), jnp.where(first, far, places)])
    pos_ids, seg_ids = places[:, 0], places[:, 1]

    all_tokens = block.gather_block(own_tokens).reshape(group_rows, width)
    upstream = block.gather_block(own_up).reshape(group_rows, width)

    cols = jnp.concatenate(
        [
            qkv_weight.reshape(near, 8, 3 * head_dim),
            jnp.swapaxes(fc1_weight.reshape(near, count, 8, units), 1, 2).reshape(near, 8, -1),
        ],
        axis=2,
    )
    cols = block.exchange(jnp.swapaxes(cols, 0, 1))
    cols = block.gather_blocks(cols).reshape(width, -1)
    w_qkv, w_up = cols[:, : 3 * head_dim], cols[:, 3 * head_dim :]
    w_rows = jnp.concatenate([fc2_weight, block.to_heads(dense_weight)])
    w_rows = block.gather_blocks(w_rows)
    w_down = w_rows[:, :units].reshape(-1, width)
    w_dense = w_rows[:, units:].reshape(-1, width)

    normed_x, inv_std = normalize(all_tokens.astype(f32))
    normed_one = (normed_x * gain_one + shift_one).astype(bf16)
    normed_two = (normed_x * gain_two + shift_two).astype(bf16)
    seqs = group_rows // seq_len
    cosines, sines = rotary_tables(pos_ids, ROT_DIMS)
    projected = (times(normed_one, w_qkv) + b_qkv).reshape(seqs, seq_len, 3, head_dim)
    queries = rotate(projected[:, :, 0], cosines, sines, ROT_DIMS).astype(bf16)
    keys = rotate(projected[:, :, 1], cosines, sines, ROT_DIMS).astype(bf16)
    values = projected[:, :, 2].astype(bf16)
    index = jnp.arange(seq_len, dtype=jnp.int32)
    allowed = (seg_ids[:, :, None] == seg_ids[:, None, :]) & (
        index[None, None, :] <= index[None, :, None]
    )
    scores = jnp.einsum("sqd,skd->sqk", queries, keys, preferred_element_type=f32) * factor
    scores = jnp.where(allowed, scores, -1e30)
    largest = jnp.max(scores, axis=-1, keepdims=True)
    log_total = largest + jnp.log(jnp.sum(jnp.exp(scores - largest), axis=-1, keepdims=True))
    probs = jnp.exp(scores - log_total)
    probs_low = probs.astype(bf16)
    attended = jnp.einsum("sqk,skd->sqd", probs_low, values, preferred_element_type=f32)
    attended = attended.astype(bf16).reshape(group_rows, head_dim)
    hidden_pre = times(normed_two, w_up) + b_up
    gelu_cdf = 0.5 * (1.0 + jax.scipy.special.erf(hidden_pre * root_half))
    activated = (hidden_pre * gelu_cdf).astype(bf16)
    out_part = times(attended, w_dense) + times(activated, w_down)
    out_sum = block.scatter_block(out_part.astype(bf16).reshape(8, rows, width))
    output = (own_tokens.astype(f32) + out_sum + (b_dense + b_down)).astype(bf16)

    grad_down = column_products(activated, upstream)
    grad_act = times_back(upstream, w_down)
    gelu_slope = gelu_cdf + hidden_pre * jnp.exp(-0.5 * hidden_pre * hidden_pre) * inv_root_tau
    grad_hidden = (grad_act * gelu_slope).astype(bf16)
    grad_up = column_products(normed_two, grad_hidden)
    up_bias = jnp.sum(grad_hidden, axis=0, dtype=f32)
    grad_two = times_back(grad_hidden, w_up)
    grad_dense = column_products(attended, upstream)
    grad_attended = times_back(upstream, w_dense).astype(bf16).reshape(seqs, seq_len, head_dim)
    grad_probs = jnp.einsum("sqd,skd->sqk", grad_attended, values, preferred_element_type=f32)
    row_terms = jnp.sum(probs * grad_probs, axis=-1, keepdims=True)
    grad_scores = (probs * (grad_probs - row_terms)).astype(bf16)
    grad_queries = (
        jnp.einsum("sqk,skd->sqd", grad_scores, keys, preferred_element_type=f32) * factor
    )
    grad_keys = (
        jnp.einsum("sqk,sqd->skd", grad_scores, queries, preferred_element_type=f32) * factor
    )
    grad_values = jnp.einsum("sqk,sqd->skd", probs_low, grad_attended, preferred_element_type=f32)
    grad_projected = jnp.concatenate(
        [
            rotate(grad_queries, cosines, -sines, ROT_DIMS),
            rotate(grad_keys, cosines, -sines, ROT_DIMS),
            grad_values,
        ],
        axis=-1,
    )
    grad_projected = grad_projected.astype(bf16).reshape(group_rows, 3 * head_dim)
    grad_qkv = column_products(normed_one, grad_projected)
    qkv_bias_sum = jnp.sum(grad_projected, axis=0, dtype=f32)
    grad_one = times_back(grad_projected, w_qkv)

    rows_part = jnp.concatenate(
        [
            grad_down.astype(bf16).reshape(count, units, width),
            grad_dense.astype(bf16).reshape(count, near, width),
        ],
        axis=1,
    )
    rows_sum = block.scatter_blocks(rows_part)
    grad_fc2_weight = rows_sum[:units]
    grad_dense_weight = block.to_heads(rows_sum[units:].astype(bf16), back=True).astype(f32)
    cols_part = jnp.concatenate([grad_qkv, grad_up], axis=1).astype(bf16)
    cols_sum = block.scatter_blocks(cols_part.reshape(count, 8 * near, -1)).astype(bf16)
    cols_sum = block.exchange(cols_sum.reshape(8, near, -1))
    cols_sum = jnp.swapaxes(cols_sum, 0, 1).astype(f32)
    grad_qkv_weight = cols_sum[:, :, : 3 * head_dim].reshape(near, -1)
    grad_fc1_weight = jnp.swapaxes(
        cols_sum[:, :, 3 * head_dim :].reshape(near, 8, count, units), 1, 2
    ).reshape(near, -1)

    sums = jnp.stack(
        [
            jnp.sum(grad_one * normed_x, axis=0),
            jnp.sum(grad_one, axis=0),
            jnp.sum(grad_two * normed_x, axis=0),
            jnp.sum(grad_two, axis=0),
            jnp.sum(own_up.astype(f32), axis=0),
        ]
    )
    sums = jnp.swapaxes(sums.reshape(5, total, near), 0, 1).reshape(total, -1)
    own_sums = jnp.concatenate(
        [up_bias.reshape(count, units), qkv_bias_sum.reshape(count, -1)], axis=1
    )
    sums = block.scatter_small(sums, own_sums)
    grad_qkv_bias = block.to_heads(sums[5 * near + units :], back=True)

    grad_normed = (grad_one * gain_one + grad_two * gain_two).astype(bf16)
    grad_normed = block.scatter_block(grad_normed.reshape(8, rows, width))
    own_normed, own_std = normalize(own_tokens.astype(f32))
    grad_tokens = own_up.astype(f32) + own_std * (
        grad_normed
        - jnp.mean(grad_normed, axis=-1, keepdims=True)
        - own_normed * jnp.mean(grad_normed * own_normed, axis=-1, keepdims=True)
    )
    return (
        output.reshape(tokens.shape),
        grad_tokens.reshape(tokens.shape),
        sums[:near],
        sums[near : 2 * near],
        sums[2 * near : 3 * near],
        sums[3 * near : 4 * near],
        grad_qkv_weight,
        grad_qkv_bias,
        grad_dense_weight,
        sums[4 * near : 5 * near],
        grad_fc1_weight,
        sums[5 * near : 5 * near + units],
        grad_fc2_weight,
        sums[4 * near : 5 * near],
    )


def solution(mesh):
    every = ("dp", "seq")
    token, ids, vector, matrix = P("dp", "seq", None), P("dp", None), P(every), P(every, None)
    return jax.shard_map(
        on_device,
        mesh=mesh,
        in_specs=(
            token, ids, ids, vector, vector, vector, vector, matrix, vector, matrix, vector,
            matrix, vector, matrix, vector, token,
        ),
        out_specs=(
            token, token, vector, vector, vector, vector, matrix, vector, matrix, vector,
            matrix, vector, matrix, vector,
        ),
        check_vma=False,
    )
```

```python
import functools

import jax
import jax.numpy as jnp
from jax import lax
from jax.experimental import pallas as pl
from jax.experimental.layout import Layout, with_layout_constraint
from jax.experimental.pallas import tpu as pltpu
from jax.sharding import PartitionSpec as P

HEADS = 8
ROT_DIMS = 64
AXES = ("r", "p", "seq")
VMEM_LIMIT = 60 * 1024 * 1024

root_half = 0.7071067811865476
inv_root_tau = 0.3989422804014327
bf16 = jnp.bfloat16
f32 = jnp.float32


def after(value, behind):
    return lax.optimization_barrier((value, behind))[0]


def pick(array, index):
    return lax.dynamic_index_in_dim(array, index, 0, keepdims=False)


def put(array, value, index):
    return lax.dynamic_update_index_in_dim(array, value, index, 0)


def dot(left, right, left_dim=1, right_dim=0):
    return lax.dot_general(
        left, right, (((left_dim,), (right_dim,)), ((), ())), preferred_element_type=f32
    )


def call(kernel, flops, moved, **settings):
    return pl.pallas_call(
        kernel,
        compiler_params=pltpu.CompilerParams(vmem_limit_bytes=VMEM_LIMIT),
        cost_estimate=pl.CostEstimate(flops=flops, bytes_accessed=moved, transcendentals=0),
        **settings,
    )


def place_kernel(cuts, index_ref, *refs):
    pieces, outs, (held, sems_in, sems_out) = refs[:8], refs[8:-3], refs[-3:]
    fetch = [pltpu.make_async_copy(p, held.at[k], sems_in.at[k]) for k, p in enumerate(pieces)]
    store = [
        pltpu.make_async_copy(
            held.at[k, pl.ds(start, size)], out.at[index_ref[k]], sems_out.at[k, n]
        )
        for k in range(8)
        for n, (out, (start, size)) in enumerate(zip(outs, cuts))
    ]
    for copy in fetch:
        copy.start()
    for k, copy in enumerate(fetch):
        copy.wait()
        for n in range(len(cuts)):
            store[k * len(cuts) + n].start()
    for copy in store:
        copy.wait()


def place(pieces, index, cuts):
    shape, kind = pieces[0].shape, pieces[0].dtype
    return call(
        functools.partial(place_kernel, cuts),
        0,
        4 * len(pieces) * pieces[0].size,
        in_specs=[pl.BlockSpec(memory_space=pltpu.SMEM)] + [pl.BlockSpec(memory_space=pl.ANY)] * 8,
        out_specs=[pl.BlockSpec(memory_space=pl.ANY)] * len(cuts),
        out_shape=[jax.ShapeDtypeStruct((8, size) + shape[1:], kind) for _, size in cuts],
        scratch_shapes=[
            pltpu.VMEM((8,) + shape, kind),
            pltpu.SemaphoreType.DMA((8,)),
            pltpu.SemaphoreType.DMA((8, len(cuts))),
        ],
        name="place_pieces",
    )(jnp.stack(index).astype(jnp.int32), *pieces)


def line_kernel(cuts, place_ref, own, *refs):
    outs, (held, sems_in, sems_out) = refs[6:-3], refs[-3:]
    count = held.shape[0]
    below, above = refs[: count - 1], refs[count - 1 : 2 * count - 2]
    r = place_ref[0]

    def fetch(source, step):
        return pltpu.make_async_copy(source, held.at[step], sems_in.at[step])

    def stores(step):
        row = jnp.where(r >= step, r - step, r - step + count)
        return [
            pltpu.make_async_copy(
                held.at[step, pl.ds(start, size)],
                outs[which].at[row, :, pl.ds(column, held.shape[2])],
                sems_out.at[step, n],
            )
            for n, (which, start, size, column) in enumerate(cuts)
        ]

    fetch(own, 0).start()
    for step in range(1, count):

        @pl.when(r >= step)
        def _():
            fetch(below[step - 1], step).start()

        @pl.when(r < step)
        def _():
            fetch(above[count - step - 1], step).start()

    for step in range(count):
        fetch(own, step).wait()
        for copy in stores(step):
            copy.start()
    for step in range(count):
        for copy in stores(step):
            copy.wait()


def place_line(own, below, above, r, shapes):
    count, wide = len(below) + 1, own.shape[1]
    cuts, start = [], 0
    for which, (rows, columns) in enumerate(shapes):
        for column in range(0, columns, wide):
            cuts.append((which, start, rows, column))
            start += rows
    return call(
        functools.partial(line_kernel, cuts),
        0,
        4 * count * own.size,
        in_specs=[pl.BlockSpec(memory_space=pltpu.SMEM)]
        + [pl.BlockSpec(memory_space=pl.ANY)] * (2 * count - 1),
        out_specs=[pl.BlockSpec(memory_space=pl.ANY)] * len(shapes),
        out_shape=[jax.ShapeDtypeStruct((count,) + shape, own.dtype) for shape in shapes],
        scratch_shapes=[
            pltpu.VMEM((count,) + own.shape, own.dtype),
            pltpu.SemaphoreType.DMA((count,)),
            pltpu.SemaphoreType.DMA((count, len(cuts))),
        ],
        name="place_line",
    )(r.reshape(1), own, *below, *above)


def norm_kernel(tokens, params, one, two, mean_ref, inv_ref):
    values = tokens[...].astype(f32)
    average = jnp.mean(values, axis=-1, keepdims=True)
    centred = values - average
    inv_std = lax.rsqrt(jnp.mean(centred * centred, axis=-1, keepdims=True) + 1e-05)
    normed = centred * inv_std
    one[...] = (normed * params[0:1] + params[1:2]).astype(bf16)
    two[...] = (normed * params[2:3] + params[3:4]).astype(bf16)
    mean_ref[...] = average
    inv_ref[...] = inv_std


def norms(tokens, params):
    rows, width = tokens.shape
    tile = 256
    wide = pl.BlockSpec((tile, width), lambda i: (i, 0))
    thin = pl.BlockSpec((tile, 1), lambda i: (i, 0))
    return call(
        norm_kernel,
        10 * rows * width,
        6 * rows * width,
        grid=(rows // tile,),
        in_specs=[wide, pl.BlockSpec(params.shape, lambda i: (0, 0))],
        out_specs=[wide, wide, thin, thin],
        out_shape=[
            jax.ShapeDtypeStruct((rows, width), bf16),
            jax.ShapeDtypeStruct((rows, width), bf16),
            jax.ShapeDtypeStruct((rows, 1), f32),
            jax.ShapeDtypeStruct((rows, 1), f32),
        ],
        name="norms",
    )(tokens, params)


def pack(out_ref, total_ref, start, count):
    rows, width = total_ref.shape
    high, wide = rows // count, width // count
    for block in range(count):
        for part in range(count):
            out_ref[block, start : start + high, part * wide : (part + 1) * wide] = total_ref[
                part * high : (part + 1) * high, block * wide : (block + 1) * wide
            ].astype(bf16)


def hidden_kernel(
    normed, up, w_up, w_down, b_up, act_ref, grad_ref, down_ref, up_ref, bias_ref, down_total, up_total
):
    step = pl.program_id(0)
    count = up_ref.shape[0]
    tile, width = normed.shape

    @pl.when(step == 0)
    def _():
        down_total[...] = jnp.zeros_like(down_total)
        up_total[...] = jnp.zeros_like(up_total)
        bias_ref[...] = jnp.zeros_like(bias_ref)

    part = 256
    for k in range(tile // part):
        rows = slice(k * part, (k + 1) * part)
        pre = dot(normed[rows, :], w_up[...]) + b_up[...]
        grad_act = dot(up[rows, :], w_down[...], 1, 1)
        cdf = 0.5 * (1.0 + lax.erf(pre * root_half))
        slope = cdf + pre * jnp.exp(-0.5 * pre * pre) * inv_root_tau
        act_ref[rows, :] = (pre * cdf).astype(bf16)
        grad = (grad_act * slope).astype(bf16)
        grad_ref[rows, :] = grad
        bias_ref[0:1, :] += jnp.sum(grad.astype(f32), axis=0, keepdims=True)
    cut = 512
    for k in range(width // cut):
        columns = slice(k * cut, (k + 1) * cut)
        down_total[:, columns] += dot(act_ref[...], up[:, columns], 0, 0)
        up_total[:, columns] += dot(grad_ref[...], normed[:, columns], 0, 0)

    @pl.when(step == pl.num_programs(0) - 1)
    def _():
        down_ref[...] = down_total[...].astype(bf16)
        pack(up_ref, up_total, 0, count)


def hidden_units(normed, up, w_up, w_down, b_up, count):
    rows, width = normed.shape
    units = w_up.shape[1]
    tile = 512
    wide = pl.BlockSpec((tile, width), lambda i: (i, 0))
    thin = pl.BlockSpec((tile, units), lambda i: (i, 0))
    whole = lambda shape: pl.BlockSpec(shape, lambda i: (0,) * len(shape))
    sums = (count, units // count, width)
    return call(
        hidden_kernel,
        8 * rows * width * units,
        4 * rows * width + 4 * rows * units + 8 * width * units,
        grid=(rows // tile,),
        in_specs=[wide, wide, whole(w_up.shape), whole(w_down.shape), whole((1, units))],
        out_specs=[thin, thin, whole((units, width)), whole(sums), whole((8, units))],
        out_shape=[
            jax.ShapeDtypeStruct((rows, units), bf16),
            jax.ShapeDtypeStruct((rows, units), bf16),
            jax.ShapeDtypeStruct((units, width), bf16),
            jax.ShapeDtypeStruct(sums, bf16),
            jax.ShapeDtypeStruct((8, units), f32),
        ],
        scratch_shapes=[pltpu.VMEM((units, width), f32), pltpu.VMEM((units, width), f32)],
        name="hidden_units",
    )(normed, up, w_up, w_down, b_up)


def turn(vectors, tables, sign):
    cosines, ahead, behind = tables
    lanes = cosines.shape[1]
    half = ROT_DIMS // 2
    first = vectors[:, :lanes]
    mixed = pltpu.roll(first, lanes - half, 1) * ahead + pltpu.roll(first, half, 1) * behind
    return jnp.concatenate([first * cosines + sign * mixed, vectors[:, lanes:]], axis=1)


def heads_kernel(
    normed, up, w_qkv, b_qkv, w_dense, cosines, ahead, behind, seg_row, seg_col,
    att_ref, grad_ref, sums_ref, bias_ref,
    queries, keys, values, grad_att, grad_keys, grad_values, qkv_total, dense_total,
):
    step = pl.program_id(0)
    count = sums_ref.shape[0]
    length, width = normed.shape
    head = att_ref.shape[1]
    factor = head ** (-0.5)
    part = 256

    @pl.when(step == 0)
    def _():
        qkv_total[...] = jnp.zeros_like(qkv_total)
        dense_total[...] = jnp.zeros_like(dense_total)
        bias_ref[...] = jnp.zeros_like(bias_ref)

    def tables(rows):
        return cosines[rows, :], ahead[rows, :], behind[rows, :]

    for k in range(length // part):
        rows = slice(k * part, (k + 1) * part)
        projected = dot(normed[rows, :], w_qkv[...]) + b_qkv[...]
        queries[rows, :] = turn(projected[:, :head], tables(rows), 1.0).astype(bf16)
        keys[rows, :] = turn(projected[:, head : 2 * head], tables(rows), 1.0).astype(bf16)
        values[rows, :] = projected[:, 2 * head :].astype(bf16)
        grad_att[rows, :] = dot(up[rows, :], w_dense[...], 1, 1).astype(bf16)

    grad_keys[...] = jnp.zeros_like(grad_keys)
    grad_values[...] = jnp.zeros_like(grad_values)
    for k in range(length // part):
        rows, seen = slice(k * part, (k + 1) * part), slice(0, (k + 1) * part)
        seen_len = (k + 1) * part
        place_q = k * part + lax.broadcasted_iota(jnp.int32, (part, seen_len), 0)
        place_k = lax.broadcasted_iota(jnp.int32, (part, seen_len), 1)
        allowed = (seg_col[rows, :] == seg_row[:, seen]) & (place_k <= place_q)
        scores = jnp.where(allowed, dot(queries[rows, :], keys[seen, :], 1, 1) * factor, -1e30)
        expo = jnp.exp(scores - jnp.max(scores, axis=-1, keepdims=True))
        probs = expo * (1.0 / jnp.sum(expo, axis=-1, keepdims=True))
        probs_low = probs.astype(bf16)
        att_ref[rows, :] = dot(probs_low, values[seen, :]).astype(bf16)
        grad_probs = dot(grad_att[rows, :], values[seen, :], 1, 1)
        row_terms = jnp.sum(probs * grad_probs, axis=-1, keepdims=True)
        grad_scores = (probs * (grad_probs - row_terms)).astype(bf16)
        grad_queries = dot(grad_scores, keys[seen, :]) * factor
        grad_ref[rows, :head] = turn(grad_queries, tables(rows), -1.0).astype(bf16)
        grad_keys[seen, :] += dot(grad_scores, queries[rows, :], 0, 0)
        grad_values[seen, :] += dot(probs_low, grad_att[rows, :], 0, 0)
    for k in range(length // part):
        rows = slice(k * part, (k + 1) * part)
        grad_ref[rows, head : 2 * head] = turn(
            grad_keys[rows, :] * factor, tables(rows), -1.0
        ).astype(bf16)
        grad_ref[rows, 2 * head :] = grad_values[rows, :].astype(bf16)
        bias_ref[0:1, :] += jnp.sum(grad_ref[rows, :].astype(f32), axis=0, keepdims=True)
    cut = 512
    for k in range(width // cut):
        columns = slice(k * cut, (k + 1) * cut)
        qkv_total[:, columns] += dot(grad_ref[...], normed[:, columns], 0, 0)
        dense_total[:, columns] += dot(att_ref[...], up[:, columns], 0, 0)

    @pl.when(step == pl.num_programs(0) - 1)
    def _():
        high = head // count
        for block in range(count):
            sums_ref[block, 0:high, :] = dense_total[block * high : (block + 1) * high, :].astype(
                bf16
            )
        pack(sums_ref, qkv_total, high, count)


def one_head(normed, up, w_qkv, b_qkv, w_dense, tables, seg_row, seg_col, length, count):
    rows, width = normed.shape
    head = w_dense.shape[0]
    lanes = tables[0].shape[1]
    wide = pl.BlockSpec((length, width), lambda i: (i, 0))
    thin = lambda columns: pl.BlockSpec((length, columns), lambda i: (i, 0))
    whole = lambda shape: pl.BlockSpec(shape, lambda i: (0,) * len(shape))
    sums = (count, 4 * head // count, width)
    return call(
        heads_kernel,
        20 * rows * width * head,
        4 * rows * width + 16 * width * head,
        grid=(rows // length,),
        in_specs=[
            wide, wide, whole(w_qkv.shape), whole(b_qkv.shape), whole(w_dense.shape),
            thin(lanes), thin(lanes), thin(lanes),
            pl.BlockSpec((None, 1, length), lambda i: (i, 0, 0)), thin(1),
        ],
        out_specs=[thin(head), thin(3 * head), whole(sums), whole((8, 3 * head))],
        out_shape=[
            jax.ShapeDtypeStruct((rows, head), bf16),
            jax.ShapeDtypeStruct((rows, 3 * head), bf16),
            jax.ShapeDtypeStruct(sums, bf16),
            jax.ShapeDtypeStruct((8, 3 * head), f32),
        ],
        scratch_shapes=[pltpu.VMEM((length, head), bf16)] * 4
        + [pltpu.VMEM((length, head), f32)] * 2
        + [pltpu.VMEM((3 * head, width), f32), pltpu.VMEM((head, width), f32)],
        name="one_head",
    )(normed, up, w_qkv, b_qkv, w_dense, *tables, seg_row, seg_col)


def out_kernel(core_ref, att, act, w_dense, w_down, out_ref):
    total = dot(att[...], w_dense[...])
    total += dot(act[...], w_down[...])
    out_ref[...] = total.astype(bf16)


def out_terms(core, att, act, w_dense, w_down, rows):
    width = w_dense.shape[1]
    tile = lambda array: pl.BlockSpec((rows, array.shape[1]), lambda i, c: (2 * i + c[0], 0))
    whole = lambda array: pl.BlockSpec(array.shape, lambda i, c: (0, 0))
    inner = w_dense.shape[0] + w_down.shape[0]
    return call(
        out_kernel,
        8 * rows * inner * width,
        2 * inner * width + 8 * rows * (inner + width),
        grid_spec=pltpu.PrefetchScalarGridSpec(
            num_scalar_prefetch=1,
            grid=(4,),
            in_specs=[tile(a) for a in (att, act)] + [whole(w) for w in (w_dense, w_down)],
            out_specs=pl.BlockSpec((None, rows, width), lambda i, c: (i, 0, 0)),
        ),
        out_shape=jax.ShapeDtypeStruct((4, rows, width), bf16),
        name="out_terms",
    )(core.reshape(1), att, act, w_dense, w_down)


def back_kernel(
    core_ref, tokens, mean, inv_std, params, grad_qkv, grad_hidden,
    w_qkv, w_up, out_ref, sums_ref,
):
    width = tokens.shape[1]

    @pl.when(pl.program_id(0) == 0)
    def _():
        sums_ref[...] = jnp.zeros_like(sums_ref)

    cut = 512
    for k in range(width // cut):
        columns = slice(k * cut, (k + 1) * cut)
        one = dot(grad_qkv[...], w_qkv[columns, :], 1, 1)
        two = dot(grad_hidden[...], w_up[columns, :], 1, 1)
        normed = (tokens[:, columns].astype(f32) - mean[...]) * inv_std[...]
        sums_ref[0:1, columns] += jnp.sum(one * normed, axis=0, keepdims=True)
        sums_ref[1:2, columns] += jnp.sum(one, axis=0, keepdims=True)
        sums_ref[2:3, columns] += jnp.sum(two * normed, axis=0, keepdims=True)
        sums_ref[3:4, columns] += jnp.sum(two, axis=0, keepdims=True)
        out_ref[:, columns] = (one * params[0:1, columns] + two * params[2:3, columns]).astype(
            bf16
        )


def back_terms(core, tokens, stats, params, grad_qkv, grad_hidden, w_qkv, w_up, rows):
    width = tokens.shape[1]
    tile = lambda array: pl.BlockSpec((rows, array.shape[1]), lambda i, c: (2 * i + c[0], 0))
    whole = lambda array: pl.BlockSpec(array.shape, lambda i, c: (0, 0))
    inner = w_qkv.shape[1] + w_up.shape[1]
    ins = [(tile, a) for a in (tokens, *stats)] + [(whole, params)]
    ins += [(tile, a) for a in (grad_qkv, grad_hidden)] + [(whole, a) for a in (w_qkv, w_up)]
    return call(
        back_kernel,
        8 * rows * inner * width,
        2 * inner * width + 8 * rows * (inner + 2 * width),
        grid_spec=pltpu.PrefetchScalarGridSpec(
            num_scalar_prefetch=1,
            grid=(4,),
            in_specs=[spec(array) for spec, array in ins],
            out_specs=[
                pl.BlockSpec((None, rows, width), lambda i, c: (i, 0, 0)),
                pl.BlockSpec((8, width), lambda i, c: (0, 0)),
            ],
        ),
        out_shape=[
            jax.ShapeDtypeStruct((4, rows, width), bf16),
            jax.ShapeDtypeStruct((8, width), f32),
        ],
        name="back_terms",
    )(core.reshape(1), *(array for _, array in ins))


class Block:
    def __init__(self):
        self.blocks = lax.axis_size("r")
        self.total = self.blocks * 8
        self.r = lax.axis_index("r")
        self.g = lax.axis_index("p") * 4 + lax.axis_index("seq")
        self.pq = self.g // 2
        self.c = self.g % 2

    def swap(self, array, mask):
        return lax.ppermute(array, AXES, [(i, i ^ mask) for i in range(self.total)])

    def along(self, array, step, low, high):
        pairs = [
            (8 * r + g, 8 * ((r + step) % self.blocks) + g)
            for r in range(low, high)
            for g in range(8)
        ]
        return lax.ppermute(array, AXES, pairs)

    def gather_blocks(self, array, behind=()):
        return lax.all_gather(after(array, behind), "r")

    def scatter_blocks(self, parts):
        flat = parts.reshape((-1,) + parts.shape[2:])
        flat = with_layout_constraint(flat, Layout((0, 1)))
        return lax.psum_scatter(flat, "r", scatter_dimension=0, tiled=True)

    def line_small(self, array):
        count = self.blocks
        out = put(jnp.zeros((count,) + array.shape, array.dtype), array, self.r)
        for step in range(1, count):
            out = put(out, self.along(array, step, 0, count), (self.r - step) % count)
        return out

    def to_heads(self, array, back=False):
        pairs = [(h * self.blocks + r, r * 8 + h) for h in range(8) for r in range(self.blocks)]
        if back:
            pairs = [(b, a) for a, b in pairs]
        return lax.ppermute(array, AXES, pairs)


class Split:
    def __init__(self, block, kept, sent):
        self.block = block
        half = kept.shape[1] // 2
        terms = kept.astype(f32) + sent.astype(f32)
        terms = terms.astype(bf16).reshape((2, 2) + kept.shape[1:])
        self.one, self.two = terms[:, :, :half], jnp.swapaxes(terms, 0, 1)[:, :, half:]

    def round_one(self):
        block = self.block
        p, q = block.pq // 2, block.pq % 2
        self.one_in = block.swap(pick(self.one, 1 - p), 4)
        self.two_in = block.swap(pick(self.two, 1 - q), 2)

    def round_two(self):
        block = self.block
        p, q = block.pq // 2, block.pq % 2
        one = pick(self.one, p).astype(f32) + self.one_in.astype(f32)
        two = pick(self.two, q).astype(f32) + self.two_in.astype(f32)
        self.one_in = block.swap(pick(one, 1 - q).astype(bf16), 2)
        self.two_in = block.swap(pick(two, 1 - p).astype(bf16), 4)
        self.one, self.two = pick(one, q), pick(two, p)

    def finish(self):
        return jnp.concatenate(
            [self.one + self.one_in.astype(f32), self.two + self.two_in.astype(f32)]
        )


class Sums:
    def __init__(self, block, block_parts, own_parts):
        self.block, self.own_parts = block, own_parts
        parts = block_parts.reshape(block.blocks, 2, 2, 2, -1)
        self.parts = parts.transpose(3, 1, 2, 0, 4)

    def round(self, mask):
        block = self.block
        bit = {4: block.pq // 2, 2: block.pq % 2, 1: block.c}[mask]
        self.parts = pick(self.parts, bit) + block.swap(pick(self.parts, 1 - bit), mask)

    def finish(self):
        block, count = self.block, self.block.blocks
        parts = jnp.concatenate([self.parts, self.own_parts], axis=-1)
        total = pick(parts, block.r)
        for step in range(1, count):
            sent = block.along(pick(parts, (block.r + step) % count), step, 0, count)
            total = total + sent
        return total


class Rows:
    def __init__(self, block, array):
        self.block, self.mine = block, [array]

    def round_one(self):
        self.mine += [self.block.swap(self.mine[0], 2 * mask) for mask in (1, 2, 3)]

    def finish(self, cuts):
        block = self.block
        others = [block.swap(piece, 1) for piece in self.mine]
        index = [(block.pq ^ mask) * 2 + block.c for mask in range(4)]
        index += [(block.pq ^ mask) * 2 + 1 - block.c for mask in range(4)]
        return place(self.mine + others, index, cuts)


class Line:
    def __init__(self, block, arrays, wide):
        self.block, self.short = block, block.blocks == 4
        self.shapes = tuple(a.shape for a in arrays)
        if self.short:
            cut = [jnp.swapaxes(a.reshape(a.shape[0], -1, wide), 0, 1) for a in arrays]
            arrays = [jnp.concatenate([c.reshape(-1, wide) for c in cut])]
        self.arrays, self.below, self.above = arrays, [], []

    def round(self):
        if not self.short:
            return
        step = len(self.below)
        below, above = (self.below + self.arrays)[-1], (self.above + self.arrays)[-1]
        if step:
            below, above = self.below[-1], self.above[-1]
        self.below = self.below + [self.block.along(below, 1, step, 3)]
        self.above = self.above + [self.block.along(above, -1, 1, 4 - step)]

    def finish(self):
        if not self.short:
            return [lax.all_gather(a, "r") for a in self.arrays]
        return place_line(
            self.arrays[0], self.below, self.above, self.block.r, self.shapes
        )


def phase(*movers):
    held = [
        {k: v for k, v in vars(m).items() if k not in ("block", "short", "shapes")}
        if not isinstance(m, (jax.Array, list, tuple)) else m
        for m in movers
    ]
    held = lax.optimization_barrier(held)
    for mover, values in zip(movers, held):
        if not isinstance(mover, (jax.Array, list, tuple)):
            vars(mover).update(values)
    return [h for m, h in zip(movers, held) if isinstance(m, (jax.Array, list, tuple))]


def rotary_tables(positions, lanes):
    half = ROT_DIMS // 2
    inverse = 10000.0 ** (-(2.0 * jnp.arange(half, dtype=f32)) / ROT_DIMS)
    angles = positions[..., None] * inverse
    cosines, sines = jnp.cos(angles), jnp.sin(angles)
    zeros = jnp.zeros_like(sines)
    rest = positions.shape + (lanes - ROT_DIMS,)
    return [
        jnp.concatenate([cosines, cosines, jnp.ones(rest, f32)], axis=-1),
        jnp.concatenate([-sines, zeros, jnp.zeros(rest, f32)], axis=-1),
        jnp.concatenate([zeros, sines, jnp.zeros(rest, f32)], axis=-1),
    ]


def on_device(
    tokens,
    segments,
    positions,
    ln1_gain,
    ln1_bias,
    ln2_gain,
    ln2_bias,
    qkv_weight,
    qkv_bias,
    dense_weight,
    dense_bias,
    fc1_weight,
    fc1_bias,
    fc2_weight,
    fc2_bias,
    cotangent,
):
    block = Block()
    count, total = block.blocks, block.total
    num_seqs, pos_dev, width = tokens.shape
    seq_len = segments.shape[1]
    rows = num_seqs * pos_dev
    group_rows = 8 * rows
    head_dim = width // HEADS
    near = qkv_weight.shape[0]
    units = fc2_weight.shape[0]
    half = units // 2
    own_tokens = tokens.reshape(rows, width)
    own_up = cotangent.reshape(rows, width)

    group = ("p", "seq")
    w_down = block.gather_blocks(fc2_weight)
    cols = [
        jnp.swapaxes(fc1_weight.reshape(near, count, 8, units), 1, 2).reshape(near, 8, -1),
        qkv_weight.reshape(near, 8, 3 * head_dim),
    ]
    cols = jnp.swapaxes(jnp.concatenate(cols, axis=2), 0, 1)
    cols = lax.all_to_all(cols, group, 0, 0, tiled=True).reshape(8 * near, -1)
    cut = count * units
    w_up = block.gather_blocks(cols[:, :cut])
    vectors = [ln1_gain, ln1_bias, ln2_gain, ln2_bias, dense_bias, fc2_bias, qkv_bias, fc1_bias]
    small = jnp.concatenate([v.reshape(-1, near) for v in vectors])
    kinds = small.shape[0]
    places = jnp.concatenate([positions, segments]).astype(f32)[None]
    cols, small, places, up, dense_rows = phase(
        cols, small.astype(f32), places, own_up, dense_weight
    )
    upstream = Rows(block, up)
    upstream.round_one()
    far = block.swap(places, 4)
    dense_rows = block.to_heads(dense_rows)
    far, dense_rows, small = phase(far, dense_rows, small)
    small = block.line_small(small)
    small_rows = jnp.zeros((16 * width,), bf16).at[: small.size].set(small.reshape(-1).astype(bf16))
    tokens_block = Rows(block, jnp.concatenate([own_tokens, small_rows.reshape(16, width)]))
    w_dense = Line(block, [dense_rows], width)
    phase(upstream, tokens_block, w_dense)
    tokens_block.round_one()
    w_dense.round()
    first = block.pq // 2 == 0
    places = jnp.concatenate([jnp.where(first, places, far), jnp.where(first, far, places)])
    tables = [t.reshape(group_rows, -1) for t in rotary_tables(places[:, 0], 128)]
    seg_row = places[:, 1:]
    seg_col = places[:, 1].reshape(group_rows, 1)
    upstream, = upstream.finish([(0, rows)])
    upstream = upstream.reshape(group_rows, width)
    tables, seg_row, seg_col, upstream = phase(
        tokens_block, w_dense, tables, seg_row, seg_col, upstream
    )
    w_dense.round()
    all_tokens, small = tokens_block.finish([(0, rows), (rows, 16)])
    all_tokens = all_tokens.reshape(group_rows, width)
    all_tokens, small = phase(w_dense, all_tokens, small)
    w_dense.round()
    small = small.reshape(8, -1)[:, : total * kinds * near // 8].reshape(8, count, kinds, near)
    small = jnp.swapaxes(small, 0, 1).reshape(total, kinds, near).astype(f32)
    params = jnp.swapaxes(small[:, :6], 0, 1).reshape(6, width)
    out_bias = params[4] + params[5]
    params = jnp.concatenate([params, jnp.zeros((2, width), f32)])
    b_qkv = pick(small[:, 6:9].reshape(8, 1, 3 * head_dim), block.g)
    b_up = lax.dynamic_index_in_dim(
        small[:, 9:].reshape(count, 8, units), block.g, 1, keepdims=False
    ).reshape(1, -1)
    normed_one, normed_two, *stats = norms(all_tokens, params)
    normed_one, normed_two, stats, w_up, w_down = phase(
        w_dense, normed_one, normed_two, stats, w_up, w_down
    )
    w_up, w_down = w_up.reshape(width, -1), w_down.reshape(-1, width)
    w_qkv = block.gather_blocks(cols[:, cut:], w_up[:16]).reshape(width, -1)

    activated, grad_hidden, down_parts, up_parts, up_bias = hidden_units(
        normed_two, upstream, w_up, w_down, b_up, count
    )
    up_sum = block.scatter_blocks(up_parts)
    normed_one, activated, w_qkv = phase(w_dense, normed_one, activated, w_qkv)
    w_dense = w_dense.finish()[0].reshape(-1, width)

    attended, grad_projected, parts, bias = one_head(
        normed_one, upstream, w_qkv, b_qkv, w_dense, tables, seg_row, seg_col, seq_len, count
    )
    own_sums = jnp.concatenate([b[0].reshape(count, -1) for b in (up_bias, bias)], axis=1)
    heads_sum = block.scatter_blocks(parts)
    attended, grad_projected, own_sums, down_parts, _ = phase(
        attended, grad_projected, own_sums, down_parts, parts
    )
    down_sum = block.scatter_blocks(down_parts.reshape(count, units, width))

    core = block.c.astype(jnp.int32)
    back = functools.partial(
        back_terms, tokens=all_tokens, stats=stats, params=params, grad_qkv=grad_projected,
        grad_hidden=grad_hidden, w_qkv=w_qkv, w_up=w_up, rows=rows,
    )
    sent, sums_sent = back(1 - core)
    sent = block.swap(sent, 1)
    kept, sums_kept = back(core)
    sums = jnp.concatenate(
        [(sums_sent + sums_kept)[:4], jnp.sum(own_up.astype(f32), axis=0, keepdims=True)]
    )
    sums = jnp.swapaxes(sums.reshape(5, total, near), 0, 1).reshape(total, -1)
    sums = Sums(block, sums, own_sums)
    grad_normed = Split(block, kept, sent)
    attended, = phase(grad_normed, sums, attended)

    grad_normed.round_one()
    sums.round(1)
    sent = block.swap(out_terms(1 - core, attended, activated, w_dense, w_down, rows), 1)
    attended, sent = phase(grad_normed, sums, attended, sent)

    grad_normed.round_two()
    sums.round(4)
    kept = out_terms(core, attended, activated, w_dense, w_down, rows)
    out_sum = Split(block, kept, sent)
    up_sum, = phase(grad_normed, sums, out_sum, up_sum)

    out_sum.round_one()
    sums.round(2)
    parts = up_sum.reshape(units, count, 8, near).transpose(2, 3, 1, 0)
    parts = lax.all_to_all(parts, group, 0, 0, tiled=True)
    grad_normed = grad_normed.finish()
    grad_normed, = phase(out_sum, sums, grad_normed)

    out_sum.round_two()
    sums = sums.finish()
    grad_fc1_weight = parts.transpose(1, 2, 0, 3).reshape(near, -1).astype(f32)
    sums, heads_sum, grad_fc1_weight = phase(out_sum, sums, heads_sum, grad_fc1_weight)

    part = heads_sum[near:].reshape(-1, count, 8, near).transpose(2, 3, 1, 0)
    part = lax.all_to_all(part.reshape(8, near, -1), group, 0, 0, tiled=True)
    grad_dense_weight = block.to_heads(heads_sum[:near], back=True).astype(f32)
    grad_qkv_bias = block.to_heads(sums[5 * near + units :], back=True)
    output = (own_tokens.astype(f32) + out_sum.finish() + out_bias).astype(bf16)
    grad_qkv_weight = jnp.swapaxes(part, 0, 1).reshape(near, -1).astype(f32)
    output, grad_qkv_bias, grad_qkv_weight, grad_dense_weight, down_sum = phase(
        output, grad_qkv_bias, grad_qkv_weight, grad_dense_weight, down_sum
    )
    grad_fc2_weight = down_sum.astype(f32)

    grad_normed = grad_normed.astype(f32)
    values = own_tokens.astype(f32)
    own_up_wide = own_up.astype(f32)
    centred = values - jnp.mean(values, axis=-1, keepdims=True)
    own_std = lax.rsqrt(jnp.mean(centred * centred, axis=-1, keepdims=True) + 1e-05)
    own_normed = centred * own_std
    grad_tokens = own_up_wide + own_std * (
        grad_normed
        - jnp.mean(grad_normed, axis=-1, keepdims=True)
        - own_normed * jnp.mean(grad_normed * own_normed, axis=-1, keepdims=True)
    )

    return (
        output.reshape(tokens.shape),
        grad_tokens.reshape(tokens.shape),
        sums[:near],
        sums[near : 2 * near],
        sums[2 * near : 3 * near],
        sums[3 * near : 4 * near],
        grad_qkv_weight,
        grad_qkv_bias,
        grad_dense_weight,
        sums[4 * near : 5 * near],
        grad_fc1_weight,
        sums[5 * near : 5 * near + units],
        grad_fc2_weight,
        sums[4 * near : 5 * near],
    )


def solution(mesh):
    blocks = mesh.shape["dp"] // 2
    mesh = jax.sharding.Mesh(mesh.devices.reshape(blocks, 2, -1), AXES)
    dp = ("r", "p")
    token, ids, vector, matrix = P(dp, "seq", None), P(dp, None), P(AXES), P(AXES, None)
    return jax.shard_map(
        on_device,
        mesh=mesh,
        in_specs=(
            token, ids, ids, vector, vector, vector, vector, matrix, vector, matrix, vector,
            matrix, vector, matrix, vector, token,
        ),
        out_specs=(
            token, token, vector, vector, vector, vector, matrix, vector, matrix, vector,
            matrix, vector, matrix, vector,
        ),
        check_vma=False,
    )
```

```python
import functools

import jax
import jax.numpy as jnp
from jax import lax
from jax.experimental import pallas as pl
from jax.experimental.layout import Layout, with_layout_constraint
from jax.experimental.pallas import tpu as pltpu
from jax.sharding import PartitionSpec as P

HEADS = 8
ROT_DIMS = 64
AXES = ("r", "p", "seq")
VMEM_LIMIT = 60 * 1024 * 1024

root_half = 0.7071067811865476
inv_root_tau = 0.3989422804014327
bf16 = jnp.bfloat16
f32 = jnp.float32


def after(value, behind):
    return lax.optimization_barrier((value, behind))[0]


def pick(array, index):
    return lax.dynamic_index_in_dim(array, index, 0, keepdims=False)


def put(array, value, index):
    return lax.dynamic_update_index_in_dim(array, value, index, 0)


def dot(left, right, left_dim=1, right_dim=0):
    return lax.dot_general(
        left, right, (((left_dim,), (right_dim,)), ((), ())), preferred_element_type=f32
    )


def call(kernel, flops, moved, **settings):
    return pl.pallas_call(
        kernel,
        compiler_params=pltpu.CompilerParams(vmem_limit_bytes=VMEM_LIMIT),
        cost_estimate=pl.CostEstimate(flops=flops, bytes_accessed=moved, transcendentals=0),
        **settings,
    )


def place_kernel(cuts, index_ref, *refs):
    pieces, outs, (held, sems_in, sems_out) = refs[:8], refs[8:-3], refs[-3:]
    fetch = [pltpu.make_async_copy(p, held.at[k], sems_in.at[k]) for k, p in enumerate(pieces)]
    store = [
        pltpu.make_async_copy(
            held.at[k, pl.ds(start, size)], out.at[index_ref[k]], sems_out.at[k, n]
        )
        for k in range(8)
        for n, (out, (start, size)) in enumerate(zip(outs, cuts))
    ]
    for copy in fetch:
        copy.start()
    for k, copy in enumerate(fetch):
        copy.wait()
        for n in range(len(cuts)):
            store[k * len(cuts) + n].start()
    for copy in store:
        copy.wait()


def place(pieces, index, cuts):
    shape, kind = pieces[0].shape, pieces[0].dtype
    return call(
        functools.partial(place_kernel, cuts),
        0,
        4 * len(pieces) * pieces[0].size,
        in_specs=[pl.BlockSpec(memory_space=pltpu.SMEM)] + [pl.BlockSpec(memory_space=pl.ANY)] * 8,
        out_specs=[pl.BlockSpec(memory_space=pl.ANY)] * len(cuts),
        out_shape=[jax.ShapeDtypeStruct((8, size) + shape[1:], kind) for _, size in cuts],
        scratch_shapes=[
            pltpu.VMEM((8,) + shape, kind),
            pltpu.SemaphoreType.DMA((8,)),
            pltpu.SemaphoreType.DMA((8, len(cuts))),
        ],
        name="place_pieces",
    )(jnp.stack(index).astype(jnp.int32), *pieces)


def norm_kernel(tokens, params, one, two, mean_ref, inv_ref):
    values = tokens[...].astype(f32)
    average = jnp.mean(values, axis=-1, keepdims=True)
    centred = values - average
    inv_std = lax.rsqrt(jnp.mean(centred * centred, axis=-1, keepdims=True) + 1e-05)
    normed = centred * inv_std
    one[...] = (normed * params[0:1] + params[1:2]).astype(bf16)
    two[...] = (normed * params[2:3] + params[3:4]).astype(bf16)
    mean_ref[...] = average
    inv_ref[...] = inv_std


def norms(tokens, params):
    rows, width = tokens.shape
    tile = 256
    wide = pl.BlockSpec((tile, width), lambda i: (i, 0))
    thin = pl.BlockSpec((tile, 1), lambda i: (i, 0))
    return call(
        norm_kernel,
        10 * rows * width,
        6 * rows * width,
        grid=(rows // tile,),
        in_specs=[wide, pl.BlockSpec(params.shape, lambda i: (0, 0))],
        out_specs=[wide, wide, thin, thin],
        out_shape=[
            jax.ShapeDtypeStruct((rows, width), bf16),
            jax.ShapeDtypeStruct((rows, width), bf16),
            jax.ShapeDtypeStruct((rows, 1), f32),
            jax.ShapeDtypeStruct((rows, 1), f32),
        ],
        name="norms",
    )(tokens, params)


def pack(out_ref, total_ref, start, count):
    rows, width = total_ref.shape
    high, wide = rows // count, width // count
    for block in range(count):
        for part in range(count):
            out_ref[block, start : start + high, part * wide : (part + 1) * wide] = total_ref[
                part * high : (part + 1) * high, block * wide : (block + 1) * wide
            ].astype(bf16)


def hidden_kernel(
    normed, up, w_up, w_down, b_up, act_ref, grad_ref, down_ref, up_ref, bias_ref, down_total, up_total
):
    step = pl.program_id(0)
    count = up_ref.shape[0]
    tile, width = normed.shape

    @pl.when(step == 0)
    def _():
        down_total[...] = jnp.zeros_like(down_total)
        up_total[...] = jnp.zeros_like(up_total)
        bias_ref[...] = jnp.zeros_like(bias_ref)

    part = 256
    for k in range(tile // part):
        rows = slice(k * part, (k + 1) * part)
        pre = dot(normed[rows, :], w_up[...]) + b_up[...]
        grad_act = dot(up[rows, :], w_down[...], 1, 1)
        cdf = 0.5 * (1.0 + lax.erf(pre * root_half))
        slope = cdf + pre * jnp.exp(-0.5 * pre * pre) * inv_root_tau
        act_ref[rows, :] = (pre * cdf).astype(bf16)
        grad = (grad_act * slope).astype(bf16)
        grad_ref[rows, :] = grad
        bias_ref[0:1, :] += jnp.sum(grad.astype(f32), axis=0, keepdims=True)
    cut = 512
    for k in range(width // cut):
        columns = slice(k * cut, (k + 1) * cut)
        down_total[:, columns] += dot(act_ref[...], up[:, columns], 0, 0)
        up_total[:, columns] += dot(grad_ref[...], normed[:, columns], 0, 0)

    @pl.when(step == pl.num_programs(0) - 1)
    def _():
        down_ref[...] = down_total[...].astype(bf16)
        pack(up_ref, up_total, 0, count)


def hidden_units(normed, up, w_up, w_down, b_up, count):
    rows, width = normed.shape
    units = w_up.shape[1]
    tile = 512
    wide = pl.BlockSpec((tile, width), lambda i: (i, 0))
    thin = pl.BlockSpec((tile, units), lambda i: (i, 0))
    whole = lambda shape: pl.BlockSpec(shape, lambda i: (0,) * len(shape))
    sums = (count, units // count, width)
    return call(
        hidden_kernel,
        8 * rows * width * units,
        4 * rows * width + 4 * rows * units + 8 * width * units,
        grid=(rows // tile,),
        in_specs=[wide, wide, whole(w_up.shape), whole(w_down.shape), whole((1, units))],
        out_specs=[thin, thin, whole((units, width)), whole(sums), whole((8, units))],
        out_shape=[
            jax.ShapeDtypeStruct((rows, units), bf16),
            jax.ShapeDtypeStruct((rows, units), bf16),
            jax.ShapeDtypeStruct((units, width), bf16),
            jax.ShapeDtypeStruct(sums, bf16),
            jax.ShapeDtypeStruct((8, units), f32),
        ],
        scratch_shapes=[pltpu.VMEM((units, width), f32), pltpu.VMEM((units, width), f32)],
        name="hidden_units",
    )(normed, up, w_up, w_down, b_up)


def turn(vectors, tables, sign):
    cosines, ahead, behind = tables
    lanes = cosines.shape[1]
    half = ROT_DIMS // 2
    first = vectors[:, :lanes]
    mixed = pltpu.roll(first, lanes - half, 1) * ahead + pltpu.roll(first, half, 1) * behind
    return jnp.concatenate([first * cosines + sign * mixed, vectors[:, lanes:]], axis=1)


def heads_kernel(
    normed, up, w_qkv, b_qkv, w_dense, cosines, ahead, behind, seg_row, seg_col,
    att_ref, grad_ref, dense_ref, sums_ref, bias_ref,
    queries, keys, values, grad_att, grad_keys, grad_values, qkv_total, dense_total,
):
    step = pl.program_id(0)
    count = sums_ref.shape[0]
    length, width = normed.shape
    head = att_ref.shape[1]
    factor = head ** (-0.5)
    part = 256

    @pl.when(step == 0)
    def _():
        qkv_total[...] = jnp.zeros_like(qkv_total)
        dense_total[...] = jnp.zeros_like(dense_total)
        bias_ref[...] = jnp.zeros_like(bias_ref)

    def tables(rows):
        return cosines[rows, :], ahead[rows, :], behind[rows, :]

    for k in range(length // part):
        rows = slice(k * part, (k + 1) * part)
        projected = dot(normed[rows, :], w_qkv[...]) + b_qkv[...]
        queries[rows, :] = turn(projected[:, :head], tables(rows), 1.0).astype(bf16)
        keys[rows, :] = turn(projected[:, head : 2 * head], tables(rows), 1.0).astype(bf16)
        values[rows, :] = projected[:, 2 * head :].astype(bf16)
        grad_att[rows, :] = dot(up[rows, :], w_dense[...], 1, 1).astype(bf16)

    grad_keys[...] = jnp.zeros_like(grad_keys)
    grad_values[...] = jnp.zeros_like(grad_values)
    for k in range(length // part):
        rows, seen = slice(k * part, (k + 1) * part), slice(0, (k + 1) * part)
        seen_len = (k + 1) * part
        place_q = k * part + lax.broadcasted_iota(jnp.int32, (part, seen_len), 0)
        place_k = lax.broadcasted_iota(jnp.int32, (part, seen_len), 1)
        allowed = (seg_col[rows, :] == seg_row[:, seen]) & (place_k <= place_q)
        scores = jnp.where(allowed, dot(queries[rows, :], keys[seen, :], 1, 1) * factor, -1e30)
        expo = jnp.exp(scores - jnp.max(scores, axis=-1, keepdims=True))
        probs = expo * (1.0 / jnp.sum(expo, axis=-1, keepdims=True))
        probs_low = probs.astype(bf16)
        att_ref[rows, :] = dot(probs_low, values[seen, :]).astype(bf16)
        grad_probs = dot(grad_att[rows, :], values[seen, :], 1, 1)
        row_terms = jnp.sum(probs * grad_probs, axis=-1, keepdims=True)
        grad_scores = (probs * (grad_probs - row_terms)).astype(bf16)
        grad_queries = dot(grad_scores, keys[seen, :]) * factor
        grad_ref[rows, :head] = turn(grad_queries, tables(rows), -1.0).astype(bf16)
        grad_keys[seen, :] += dot(grad_scores, queries[rows, :], 0, 0)
        grad_values[seen, :] += dot(probs_low, grad_att[rows, :], 0, 0)
    for k in range(length // part):
        rows = slice(k * part, (k + 1) * part)
        grad_ref[rows, head : 2 * head] = turn(
            grad_keys[rows, :] * factor, tables(rows), -1.0
        ).astype(bf16)
        grad_ref[rows, 2 * head :] = grad_values[rows, :].astype(bf16)
        bias_ref[0:1, :] += jnp.sum(grad_ref[rows, :].astype(f32), axis=0, keepdims=True)
    cut = 512
    for k in range(width // cut):
        columns = slice(k * cut, (k + 1) * cut)
        qkv_total[:, columns] += dot(grad_ref[...], normed[:, columns], 0, 0)
        dense_total[:, columns] += dot(att_ref[...], up[:, columns], 0, 0)

    @pl.when(step == pl.num_programs(0) - 1)
    def _():
        dense_ref[...] = dense_total[...].astype(bf16)
        pack(sums_ref, qkv_total, 0, count)


def one_head(normed, up, w_qkv, b_qkv, w_dense, tables, seg_row, seg_col, length, count):
    rows, width = normed.shape
    head = w_dense.shape[0]
    lanes = tables[0].shape[1]
    wide = pl.BlockSpec((length, width), lambda i: (i, 0))
    thin = lambda columns: pl.BlockSpec((length, columns), lambda i: (i, 0))
    whole = lambda shape: pl.BlockSpec(shape, lambda i: (0,) * len(shape))
    sums = (count, 3 * head // count, width)
    return call(
        heads_kernel,
        20 * rows * width * head,
        4 * rows * width + 16 * width * head,
        grid=(rows // length,),
        in_specs=[
            wide, wide, whole(w_qkv.shape), whole(b_qkv.shape), whole(w_dense.shape),
            thin(lanes), thin(lanes), thin(lanes),
            pl.BlockSpec((None, 1, length), lambda i: (i, 0, 0)), thin(1),
        ],
        out_specs=[
            thin(head), thin(3 * head), whole((head, width)), whole(sums), whole((8, 3 * head))
        ],
        out_shape=[
            jax.ShapeDtypeStruct((rows, head), bf16),
            jax.ShapeDtypeStruct((rows, 3 * head), bf16),
            jax.ShapeDtypeStruct((head, width), bf16),
            jax.ShapeDtypeStruct(sums, bf16),
            jax.ShapeDtypeStruct((8, 3 * head), f32),
        ],
        scratch_shapes=[pltpu.VMEM((length, head), bf16)] * 4
        + [pltpu.VMEM((length, head), f32)] * 2
        + [pltpu.VMEM((3 * head, width), f32), pltpu.VMEM((head, width), f32)],
        name="one_head",
    )(normed, up, w_qkv, b_qkv, w_dense, *tables, seg_row, seg_col)


def out_kernel(core_ref, att, act, w_dense, w_down, out_ref):
    total = dot(att[...], w_dense[...])
    total += dot(act[...], w_down[...])
    out_ref[...] = total.astype(bf16)


def out_terms(core, att, act, w_dense, w_down, rows):
    width = w_dense.shape[1]
    tile = lambda array: pl.BlockSpec((rows, array.shape[1]), lambda i, c: (2 * i + c[0], 0))
    whole = lambda array: pl.BlockSpec(array.shape, lambda i, c: (0, 0))
    inner = w_dense.shape[0] + w_down.shape[0]
    return call(
        out_kernel,
        8 * rows * inner * width,
        2 * inner * width + 8 * rows * (inner + width),
        grid_spec=pltpu.PrefetchScalarGridSpec(
            num_scalar_prefetch=1,
            grid=(4,),
            in_specs=[tile(a) for a in (att, act)] + [whole(w) for w in (w_dense, w_down)],
            out_specs=pl.BlockSpec((None, rows, width), lambda i, c: (i, 0, 0)),
        ),
        out_shape=jax.ShapeDtypeStruct((4, rows, width), bf16),
        name="out_terms",
    )(core.reshape(1), att, act, w_dense, w_down)


def back_kernel(
    core_ref, tokens, mean, inv_std, params, grad_qkv, grad_hidden,
    w_qkv, w_up, out_ref, sums_ref,
):
    width = tokens.shape[1]

    @pl.when(pl.program_id(0) == 0)
    def _():
        sums_ref[...] = jnp.zeros_like(sums_ref)

    cut = 512
    for k in range(width // cut):
        columns = slice(k * cut, (k + 1) * cut)
        one = dot(grad_qkv[...], w_qkv[columns, :], 1, 1)
        two = dot(grad_hidden[...], w_up[columns, :], 1, 1)
        normed = (tokens[:, columns].astype(f32) - mean[...]) * inv_std[...]
        sums_ref[0:1, columns] += jnp.sum(one * normed, axis=0, keepdims=True)
        sums_ref[1:2, columns] += jnp.sum(one, axis=0, keepdims=True)
        sums_ref[2:3, columns] += jnp.sum(two * normed, axis=0, keepdims=True)
        sums_ref[3:4, columns] += jnp.sum(two, axis=0, keepdims=True)
        out_ref[:, columns] = (one * params[0:1, columns] + two * params[2:3, columns]).astype(
            bf16
        )


def back_terms(core, tokens, stats, params, grad_qkv, grad_hidden, w_qkv, w_up, rows):
    width = tokens.shape[1]
    tile = lambda array: pl.BlockSpec((rows, array.shape[1]), lambda i, c: (2 * i + c[0], 0))
    whole = lambda array: pl.BlockSpec(array.shape, lambda i, c: (0, 0))
    inner = w_qkv.shape[1] + w_up.shape[1]
    ins = [(tile, a) for a in (tokens, *stats)] + [(whole, params)]
    ins += [(tile, a) for a in (grad_qkv, grad_hidden)] + [(whole, a) for a in (w_qkv, w_up)]
    return call(
        back_kernel,
        8 * rows * inner * width,
        2 * inner * width + 8 * rows * (inner + 2 * width),
        grid_spec=pltpu.PrefetchScalarGridSpec(
            num_scalar_prefetch=1,
            grid=(4,),
            in_specs=[spec(array) for spec, array in ins],
            out_specs=[
                pl.BlockSpec((None, rows, width), lambda i, c: (i, 0, 0)),
                pl.BlockSpec((8, width), lambda i, c: (0, 0)),
            ],
        ),
        out_shape=[
            jax.ShapeDtypeStruct((4, rows, width), bf16),
            jax.ShapeDtypeStruct((8, width), f32),
        ],
        name="back_terms",
    )(core.reshape(1), *(array for _, array in ins))


class Block:
    def __init__(self):
        self.blocks = lax.axis_size("r")
        self.total = self.blocks * 8
        self.r = lax.axis_index("r")
        self.g = lax.axis_index("p") * 4 + lax.axis_index("seq")
        self.pq = self.g // 2
        self.deal = self.blocks == 4 and lax.axis_size("seq") == 4
        self.heads = [2 * (g % 4) + g // 4 if self.deal else g for g in range(8)]
        self.c = self.g % 2

    def swap(self, array, mask):
        return lax.ppermute(array, AXES, [(i, i ^ mask) for i in range(self.total)])

    def along(self, array, step, low, high):
        pairs = [
            (8 * r + g, 8 * ((r + step) % self.blocks) + g)
            for r in range(low, high)
            for g in range(8)
        ]
        return lax.ppermute(array, AXES, pairs)

    def gather_blocks(self, array, behind=()):
        return lax.all_gather(after(array, behind), "r")

    def scatter_blocks(self, parts):
        flat = parts.reshape((-1,) + parts.shape[2:])
        flat = with_layout_constraint(flat, Layout((0, 1)))
        return lax.psum_scatter(flat, "r", scatter_dimension=0, tiled=True)

    def line_small(self, array):
        count = self.blocks
        out = put(jnp.zeros((count,) + array.shape, array.dtype), array, self.r)
        for step in range(1, count):
            out = put(out, self.along(array, step, 0, count), (self.r - step) % count)
        return out

    def to_heads(self, array, back=False):
        count = self.blocks
        pairs = [(h * count + r, r * 8 + g) for g, h in enumerate(self.heads) for r in range(count)]
        if back:
            pairs = [(b, a) for a, b in pairs]
        return lax.ppermute(array, AXES, pairs)


class Split:
    def __init__(self, block, kept, sent):
        self.block = block
        half = kept.shape[1] // 2
        p, q = block.pq // 2, block.pq % 2

        def terms(at, rows):
            return pick(kept, at)[rows].astype(f32) + pick(sent, at)[rows].astype(f32)

        one, two = slice(0, half), slice(half, None)
        self.one_out = jnp.stack([terms((1 - p) * 2 + k, one).astype(bf16) for k in (0, 1)])
        self.two_out = jnp.stack([terms(k * 2 + 1 - q, two).astype(bf16) for k in (0, 1)])
        self.one = [terms(p * 2 + 1 - q, one), terms(p * 2 + q, one)]
        self.two = [terms((1 - p) * 2 + q, two), terms(p * 2 + q, two)]

    def round_one(self):
        self.one_in = self.block.swap(self.one_out, 4)
        self.two_in = self.block.swap(self.two_out, 2)

    def prepare(self):
        p, q = self.block.pq // 2, self.block.pq % 2
        self.one_out = (self.one[0] + pick(self.one_in, 1 - q).astype(f32)).astype(bf16)
        self.two_out = (self.two[0] + pick(self.two_in, 1 - p).astype(f32)).astype(bf16)
        self.one = self.one[1] + pick(self.one_in, q).astype(f32)
        self.two = self.two[1] + pick(self.two_in, p).astype(f32)

    def round_two(self):
        self.one_in = self.block.swap(self.one_out, 2)
        self.two_in = self.block.swap(self.two_out, 4)

    def finish(self):
        return jnp.concatenate(
            [self.one + self.one_in.astype(f32), self.two + self.two_in.astype(f32)]
        )


class Sums:
    def __init__(self, block, block_parts, own_parts):
        self.block, self.own_parts = block, own_parts
        parts = block_parts.reshape(block.blocks, 2, 2, 2, -1)
        self.parts = parts.transpose(3, 1, 2, 0, 4)

    def round(self, mask):
        block = self.block
        bit = {4: block.pq // 2, 2: block.pq % 2, 1: block.c}[mask]
        self.parts = pick(self.parts, bit) + block.swap(pick(self.parts, 1 - bit), mask)

    def finish(self):
        block, count = self.block, self.block.blocks
        parts = jnp.concatenate([self.parts, self.own_parts], axis=-1)
        total = pick(parts, block.r)
        for step in range(1, count):
            sent = block.along(pick(parts, (block.r + step) % count), step, 0, count)
            total = total + sent
        return total


class Rows:
    def __init__(self, block, array):
        self.block, self.mine = block, [array]

    def round_one(self):
        self.mine += [self.block.swap(self.mine[0], 2 * mask) for mask in (1, 2, 3)]

    def finish(self, cuts):
        block = self.block
        others = [block.swap(piece, 1) for piece in self.mine]
        index = [(block.pq ^ mask) * 2 + block.c for mask in range(4)]
        index += [(block.pq ^ mask) * 2 + 1 - block.c for mask in range(4)]
        return place(self.mine + others, index, cuts)


def phase(*movers):
    held = [
        {k: v for k, v in vars(m).items() if k not in ("block", "short", "shapes")}
        if not isinstance(m, (jax.Array, list, tuple)) else m
        for m in movers
    ]
    held = lax.optimization_barrier(held)
    for mover, values in zip(movers, held):
        if not isinstance(mover, (jax.Array, list, tuple)):
            vars(mover).update(values)
    return [h for m, h in zip(movers, held) if isinstance(m, (jax.Array, list, tuple))]


def rotary_tables(positions, lanes):
    half = ROT_DIMS // 2
    inverse = 10000.0 ** (-(2.0 * jnp.arange(half, dtype=f32)) / ROT_DIMS)
    angles = positions[..., None] * inverse
    cosines, sines = jnp.cos(angles), jnp.sin(angles)
    zeros = jnp.zeros_like(sines)
    rest = positions.shape + (lanes - ROT_DIMS,)
    return [
        jnp.concatenate([cosines, cosines, jnp.ones(rest, f32)], axis=-1),
        jnp.concatenate([-sines, zeros, jnp.zeros(rest, f32)], axis=-1),
        jnp.concatenate([zeros, sines, jnp.zeros(rest, f32)], axis=-1),
    ]


def on_device(
    tokens,
    segments,
    positions,
    ln1_gain,
    ln1_bias,
    ln2_gain,
    ln2_bias,
    qkv_weight,
    qkv_bias,
    dense_weight,
    dense_bias,
    fc1_weight,
    fc1_bias,
    fc2_weight,
    fc2_bias,
    cotangent,
):
    block = Block()
    count, total = block.blocks, block.total
    num_seqs, pos_dev, width = tokens.shape
    seq_len = segments.shape[1]
    rows = num_seqs * pos_dev
    group_rows = 8 * rows
    head_dim = width // HEADS
    near = qkv_weight.shape[0]
    units = fc2_weight.shape[0]
    half = units // 2
    own_tokens = tokens.reshape(rows, width)
    own_up = cotangent.reshape(rows, width)

    group = ("p", "seq")
    pieces = [fc2_weight] + ([dense_weight] if block.deal else [])
    row_parts = block.gather_blocks(jnp.concatenate(pieces))
    heads = jnp.stack([qkv_weight[:, 3 * head_dim * h : 3 * head_dim * (h + 1)] for h in block.heads])
    cols = jnp.swapaxes(fc1_weight.reshape(near, count, 8, units), 1, 2).reshape(near, 8, -1)
    cols = jnp.concatenate([jnp.swapaxes(cols, 0, 1), heads], axis=2)
    cols = lax.all_to_all(cols, group, 0, 0, tiled=True).reshape(8 * near, -1)
    cut = count * units
    w_up = block.gather_blocks(cols[:, :cut])
    vectors = [ln1_gain, ln1_bias, ln2_gain, ln2_bias, dense_bias, fc2_bias, qkv_bias, fc1_bias]
    small = jnp.concatenate([v.reshape(-1, near) for v in vectors])
    kinds = small.shape[0]
    places = jnp.concatenate([positions, segments]).astype(f32)[None]
    cols, small, places, up = phase(cols, small.astype(f32), places, own_up)

    upstream = Rows(block, up)
    upstream.round_one()
    far = block.swap(places, 4)
    far, small = phase(far, small)
    small = block.line_small(small)
    small_rows = jnp.zeros((16 * width,), bf16).at[: small.size].set(small.reshape(-1).astype(bf16))
    tokens_block = Rows(block, jnp.concatenate([own_tokens, small_rows.reshape(16, width)]))
    phase(upstream, tokens_block)
    tokens_block.round_one()
    first = block.pq // 2 == 0
    places = jnp.concatenate([jnp.where(first, places, far), jnp.where(first, far, places)])
    tables = [t.reshape(group_rows, -1) for t in rotary_tables(places[:, 0], 128)]
    seg_row = places[:, 1:]
    seg_col = places[:, 1].reshape(group_rows, 1)
    upstream, = upstream.finish([(0, rows)])
    upstream = upstream.reshape(group_rows, width)
    tables, seg_row, seg_col, upstream, row_parts = phase(
        tokens_block, tables, seg_row, seg_col, upstream, row_parts
    )
    if block.deal:
        w_dense = lax.all_to_all(row_parts[:, units:], "seq", 0, 0, tiled=True)
    else:
        w_dense = block.gather_blocks(block.to_heads(dense_weight))
    w_dense, w_down = w_dense.reshape(-1, width), row_parts[:, :units].reshape(-1, width)
    all_tokens, small = tokens_block.finish([(0, rows), (rows, 16)])
    all_tokens = all_tokens.reshape(group_rows, width)
    small = small.reshape(8, -1)[:, : total * kinds * near // 8].reshape(8, count, kinds, near)
    small = jnp.swapaxes(small, 0, 1).reshape(total, kinds, near).astype(f32)
    params = jnp.swapaxes(small[:, :6], 0, 1).reshape(6, width)
    out_bias = params[4] + params[5]
    params = jnp.concatenate([params, jnp.zeros((2, width), f32)])
    b_qkv = small[:, 6:9].reshape(8, 1, 3 * head_dim)
    b_qkv = pick(jnp.stack([b_qkv[h] for h in block.heads]), block.g)
    b_up = lax.dynamic_index_in_dim(
        small[:, 9:].reshape(count, 8, units), block.g, 1, keepdims=False
    ).reshape(1, -1)
    normed_one, normed_two, *stats = norms(all_tokens, params)
    normed_one, normed_two, stats, w_up, w_down, w_dense = phase(
        normed_one, normed_two, stats, w_up, w_down, w_dense
    )
    w_up = w_up.reshape(width, -1)
    w_qkv = block.gather_blocks(cols[:, cut:], w_up[:16]).reshape(width, -1)

    activated, grad_hidden, down_parts, up_parts, up_bias = hidden_units(
        normed_two, upstream, w_up, w_down, b_up, count
    )
    up_sum = block.scatter_blocks(up_parts)
    normed_one, activated, w_qkv = phase(normed_one, activated, w_qkv)

    attended, grad_projected, dense_part, parts, bias = one_head(
        normed_one, upstream, w_qkv, b_qkv, w_dense, tables, seg_row, seg_col, seq_len, count
    )
    own_sums = jnp.concatenate([b[0].reshape(count, -1) for b in (up_bias, bias)], axis=1)
    dense_part = dense_part.reshape(count, near, width)
    if block.deal:
        dense_part = lax.all_to_all(dense_part, "seq", 0, 0, tiled=True)
    parts = jnp.concatenate([dense_part, parts], axis=1)
    heads_sum = block.scatter_blocks(parts)
    attended, grad_projected, own_sums, down_parts, _ = phase(
        attended, grad_projected, own_sums, down_parts, parts
    )
    down_sum = block.scatter_blocks(down_parts.reshape(count, units, width))

    core = block.c.astype(jnp.int32)
    back = functools.partial(
        back_terms, tokens=all_tokens, stats=stats, params=params, grad_qkv=grad_projected,
        grad_hidden=grad_hidden, w_qkv=w_qkv, w_up=w_up, rows=rows,
    )
    sent, sums_sent = back(1 - core)
    sent = block.swap(sent, 1)
    kept, sums_kept = back(core)
    sums = jnp.concatenate(
        [(sums_sent + sums_kept)[:4], jnp.sum(own_up.astype(f32), axis=0, keepdims=True)]
    )
    sums = jnp.swapaxes(sums.reshape(5, total, near), 0, 1).reshape(total, -1)
    sums = Sums(block, sums, own_sums)
    grad_normed = Split(block, kept, sent)
    up_sum, = phase(grad_normed, sums, up_sum)
    parts = up_sum.reshape(units, count, 8, near).transpose(2, 3, 1, 0)
    attended, parts = phase(grad_normed, sums, attended, parts)

    grad_normed.round_one()
    sums.round(1)
    sent = out_terms(1 - core, attended, activated, w_dense, w_down, rows)
    kept = out_terms(core, attended, activated, w_dense, w_down, rows)
    sent, kept, parts = phase(grad_normed, sums, sent, kept, parts)
    grad_normed.prepare()
    phase(grad_normed)

    grad_normed.round_two()
    sent = block.swap(sent, 1)
    sums.round(4)
    parts = lax.all_to_all(parts, group, 0, 0, tiled=True)
    out_sum = Split(block, kept, sent)
    phase(grad_normed, sums, out_sum)

    out_sum.round_one()
    sums.round(2)
    grad_normed = grad_normed.finish()
    grad_fc1_weight = parts.transpose(1, 2, 0, 3).reshape(near, -1).astype(f32)
    grad_normed, grad_fc1_weight, heads_sum = phase(
        out_sum, sums, grad_normed, grad_fc1_weight, heads_sum
    )
    out_sum.prepare()
    part = heads_sum[near:].reshape(-1, count, 8, near).transpose(2, 3, 1, 0)
    part, = phase(out_sum, part)

    out_sum.round_two()
    part = lax.all_to_all(part.reshape(8, near, -1), group, 0, 0, tiled=True)
    sums = sums.finish()
    sums, part = phase(out_sum, sums, part)

    grad_qkv_bias = block.to_heads(sums[5 * near + units :], back=True)
    output = (own_tokens.astype(f32) + out_sum.finish() + out_bias).astype(bf16)
    at = [block.heads.index(h) for h in range(8)]
    grad_qkv_weight = jnp.concatenate([part[g] for g in at], axis=1).astype(f32)
    grad_dense_weight = heads_sum[:near]
    if not block.deal:
        grad_dense_weight = block.to_heads(grad_dense_weight, back=True)
    grad_dense_weight = grad_dense_weight.astype(f32)
    output, grad_qkv_bias, grad_qkv_weight, grad_dense_weight, down_sum = phase(
        output, grad_qkv_bias, grad_qkv_weight, grad_dense_weight, down_sum
    )
    grad_fc2_weight = down_sum.astype(f32)

    grad_normed = grad_normed.astype(f32)
    values = own_tokens.astype(f32)
    own_up_wide = own_up.astype(f32)
    centred = values - jnp.mean(values, axis=-1, keepdims=True)
    own_std = lax.rsqrt(jnp.mean(centred * centred, axis=-1, keepdims=True) + 1e-05)
    own_normed = centred * own_std
    grad_tokens = own_up_wide + own_std * (
        grad_normed
        - jnp.mean(grad_normed, axis=-1, keepdims=True)
        - own_normed * jnp.mean(grad_normed * own_normed, axis=-1, keepdims=True)
    )

    return (
        output.reshape(tokens.shape),
        grad_tokens.reshape(tokens.shape),
        sums[:near],
        sums[near : 2 * near],
        sums[2 * near : 3 * near],
        sums[3 * near : 4 * near],
        grad_qkv_weight,
        grad_qkv_bias,
        grad_dense_weight,
        sums[4 * near : 5 * near],
        grad_fc1_weight,
        sums[5 * near : 5 * near + units],
        grad_fc2_weight,
        sums[4 * near : 5 * near],
    )


def solution(mesh):
    blocks = mesh.shape["dp"] // 2
    mesh = jax.sharding.Mesh(mesh.devices.reshape(blocks, 2, -1), AXES)
    dp = ("r", "p")
    token, ids, vector, matrix = P(dp, "seq", None), P(dp, None), P(AXES), P(AXES, None)
    return jax.shard_map(
        on_device,
        mesh=mesh,
        in_specs=(
            token, ids, ids, vector, vector, vector, vector, matrix, vector, matrix, vector,
            matrix, vector, matrix, vector, token,
        ),
        out_specs=(
            token, token, vector, vector, vector, vector, matrix, vector, matrix, vector,
            matrix, vector, matrix, vector,
        ),
        check_vma=False,
    )
```

```python
import functools

import jax
import jax.numpy as jnp
from jax import lax
from jax.experimental import pallas as pl
from jax.experimental.layout import Layout, with_layout_constraint
from jax.experimental.pallas import tpu as pltpu
from jax.sharding import PartitionSpec as P

HEADS = 8
ROT_DIMS = 64
AXES = ("r", "p", "seq")
VMEM_LIMIT = 60 * 1024 * 1024

root_half = 0.7071067811865476
inv_root_tau = 0.3989422804014327
bf16 = jnp.bfloat16
f32 = jnp.float32


def after(value, behind):
    return lax.optimization_barrier((value, behind))[0]


def pick(array, index):
    return lax.dynamic_index_in_dim(array, index, 0, keepdims=False)


def put(array, value, index):
    return lax.dynamic_update_index_in_dim(array, value, index, 0)


def dot(left, right, left_dim=1, right_dim=0):
    return lax.dot_general(
        left, right, (((left_dim,), (right_dim,)), ((), ())), preferred_element_type=f32
    )


def call(kernel, flops, moved, **settings):
    return pl.pallas_call(
        kernel,
        compiler_params=pltpu.CompilerParams(vmem_limit_bytes=VMEM_LIMIT),
        cost_estimate=pl.CostEstimate(flops=flops, bytes_accessed=moved, transcendentals=0),
        **settings,
    )


def place_kernel(cuts, index_ref, *refs):
    pieces, outs, (held, sems_in, sems_out) = refs[:8], refs[8:-3], refs[-3:]
    fetch = [pltpu.make_async_copy(p, held.at[k], sems_in.at[k]) for k, p in enumerate(pieces)]
    store = [
        pltpu.make_async_copy(
            held.at[k, pl.ds(start, size)], out.at[index_ref[k]], sems_out.at[k, n]
        )
        for k in range(8)
        for n, (out, (start, size)) in enumerate(zip(outs, cuts))
    ]
    for copy in fetch:
        copy.start()
    for k, copy in enumerate(fetch):
        copy.wait()
        for n in range(len(cuts)):
            store[k * len(cuts) + n].start()
    for copy in store:
        copy.wait()


def place(pieces, index, cuts):
    shape, kind = pieces[0].shape, pieces[0].dtype
    return call(
        functools.partial(place_kernel, cuts),
        0,
        4 * len(pieces) * pieces[0].size,
        in_specs=[pl.BlockSpec(memory_space=pltpu.SMEM)] + [pl.BlockSpec(memory_space=pl.ANY)] * 8,
        out_specs=[pl.BlockSpec(memory_space=pl.ANY)] * len(cuts),
        out_shape=[jax.ShapeDtypeStruct((8, size) + shape[1:], kind) for _, size in cuts],
        scratch_shapes=[
            pltpu.VMEM((8,) + shape, kind),
            pltpu.SemaphoreType.DMA((8,)),
            pltpu.SemaphoreType.DMA((8, len(cuts))),
        ],
        name="place_pieces",
    )(jnp.stack(index).astype(jnp.int32), *pieces)


def norm_kernel(tokens, params, one, two, mean_ref, inv_ref):
    values = tokens[...].astype(f32)
    average = jnp.mean(values, axis=-1, keepdims=True)
    centred = values - average
    inv_std = lax.rsqrt(jnp.mean(centred * centred, axis=-1, keepdims=True) + 1e-05)
    normed = centred * inv_std
    one[...] = (normed * params[0:1] + params[1:2]).astype(bf16)
    two[...] = (normed * params[2:3] + params[3:4]).astype(bf16)
    mean_ref[...] = average
    inv_ref[...] = inv_std


def norms(tokens, params):
    rows, width = tokens.shape
    tile = 256
    wide = pl.BlockSpec((tile, width), lambda i: (i, 0))
    thin = pl.BlockSpec((tile, 1), lambda i: (i, 0))
    return call(
        norm_kernel,
        10 * rows * width,
        6 * rows * width,
        grid=(rows // tile,),
        in_specs=[wide, pl.BlockSpec(params.shape, lambda i: (0, 0))],
        out_specs=[wide, wide, thin, thin],
        out_shape=[
            jax.ShapeDtypeStruct((rows, width), bf16),
            jax.ShapeDtypeStruct((rows, width), bf16),
            jax.ShapeDtypeStruct((rows, 1), f32),
            jax.ShapeDtypeStruct((rows, 1), f32),
        ],
        name="norms",
    )(tokens, params)


def pack(out_ref, total_ref, start, count):
    rows, width = total_ref.shape
    high, wide = rows // count, width // count
    for block in range(count):
        for part in range(count):
            out_ref[block, start : start + high, part * wide : (part + 1) * wide] = total_ref[
                part * high : (part + 1) * high, block * wide : (block + 1) * wide
            ].astype(bf16)


def hidden_kernel(
    normed, up, w_up, w_down, b_up, act_ref, grad_ref, down_ref, up_ref, bias_ref, down_total, up_total
):
    step = pl.program_id(0)
    count = up_ref.shape[0]
    tile, width = normed.shape

    @pl.when(step == 0)
    def _():
        down_total[...] = jnp.zeros_like(down_total)
        up_total[...] = jnp.zeros_like(up_total)
        bias_ref[...] = jnp.zeros_like(bias_ref)

    part = 256
    for k in range(tile // part):
        rows = slice(k * part, (k + 1) * part)
        pre = dot(normed[rows, :], w_up[...]) + b_up[...]
        grad_act = dot(up[rows, :], w_down[...], 1, 1)
        cdf = 0.5 * (1.0 + lax.erf(pre * root_half))
        slope = cdf + pre * jnp.exp(-0.5 * pre * pre) * inv_root_tau
        act_ref[rows, :] = (pre * cdf).astype(bf16)
        grad = (grad_act * slope).astype(bf16)
        grad_ref[rows, :] = grad
        bias_ref[0:1, :] += jnp.sum(grad.astype(f32), axis=0, keepdims=True)
    cut = 512
    for k in range(width // cut):
        columns = slice(k * cut, (k + 1) * cut)
        down_total[:, columns] += dot(act_ref[...], up[:, columns], 0, 0)
        up_total[:, columns] += dot(grad_ref[...], normed[:, columns], 0, 0)

    @pl.when(step == pl.num_programs(0) - 1)
    def _():
        down_ref[...] = down_total[...].astype(bf16)
        pack(up_ref, up_total, 0, count)


def hidden_units(normed, up, w_up, w_down, b_up, count):
    rows, width = normed.shape
    units = w_up.shape[1]
    tile = 512
    wide = pl.BlockSpec((tile, width), lambda i: (i, 0))
    thin = pl.BlockSpec((tile, units), lambda i: (i, 0))
    whole = lambda shape: pl.BlockSpec(shape, lambda i: (0,) * len(shape))
    sums = (count, units // count, width)
    return call(
        hidden_kernel,
        8 * rows * width * units,
        4 * rows * width + 4 * rows * units + 8 * width * units,
        grid=(rows // tile,),
        in_specs=[wide, wide, whole(w_up.shape), whole(w_down.shape), whole((1, units))],
        out_specs=[thin, thin, whole((units, width)), whole(sums), whole((8, units))],
        out_shape=[
            jax.ShapeDtypeStruct((rows, units), bf16),
            jax.ShapeDtypeStruct((rows, units), bf16),
            jax.ShapeDtypeStruct((units, width), bf16),
            jax.ShapeDtypeStruct(sums, bf16),
            jax.ShapeDtypeStruct((8, units), f32),
        ],
        scratch_shapes=[pltpu.VMEM((units, width), f32), pltpu.VMEM((units, width), f32)],
        name="hidden_units",
    )(normed, up, w_up, w_down, b_up)


def turn(vectors, tables, sign):
    cosines, ahead, behind = tables
    lanes = cosines.shape[1]
    half = ROT_DIMS // 2
    first = vectors[:, :lanes]
    mixed = pltpu.roll(first, lanes - half, 1) * ahead + pltpu.roll(first, half, 1) * behind
    return jnp.concatenate([first * cosines + sign * mixed, vectors[:, lanes:]], axis=1)


def heads_kernel(
    normed, up, w_qkv, b_qkv, w_dense, cosines, ahead, behind, seg_row, seg_col,
    att_ref, grad_ref, dense_ref, sums_ref, bias_ref,
    queries, keys, values, grad_att, grad_keys, grad_values, qkv_total, dense_total,
):
    step = pl.program_id(0)
    count = sums_ref.shape[0]
    length, width = normed.shape
    head = att_ref.shape[1]
    factor = head ** (-0.5)
    part = 256

    @pl.when(step == 0)
    def _():
        qkv_total[...] = jnp.zeros_like(qkv_total)
        dense_total[...] = jnp.zeros_like(dense_total)
        bias_ref[...] = jnp.zeros_like(bias_ref)

    def tables(rows):
        return cosines[rows, :], ahead[rows, :], behind[rows, :]

    for k in range(length // part):
        rows = slice(k * part, (k + 1) * part)
        projected = dot(normed[rows, :], w_qkv[...]) + b_qkv[...]
        queries[rows, :] = turn(projected[:, :head], tables(rows), 1.0).astype(bf16)
        keys[rows, :] = turn(projected[:, head : 2 * head], tables(rows), 1.0).astype(bf16)
        values[rows, :] = projected[:, 2 * head :].astype(bf16)
        grad_att[rows, :] = dot(up[rows, :], w_dense[...], 1, 1).astype(bf16)

    grad_keys[...] = jnp.zeros_like(grad_keys)
    grad_values[...] = jnp.zeros_like(grad_values)
    for k in range(length // part):
        rows, seen = slice(k * part, (k + 1) * part), slice(0, (k + 1) * part)
        seen_len = (k + 1) * part
        place_q = k * part + lax.broadcasted_iota(jnp.int32, (part, seen_len), 0)
        place_k = lax.broadcasted_iota(jnp.int32, (part, seen_len), 1)
        allowed = (seg_col[rows, :] == seg_row[:, seen]) & (place_k <= place_q)
        scores = jnp.where(allowed, dot(queries[rows, :], keys[seen, :], 1, 1) * factor, -1e30)
        expo = jnp.exp(scores - jnp.max(scores, axis=-1, keepdims=True))
        probs = expo * (1.0 / jnp.sum(expo, axis=-1, keepdims=True))
        probs_low = probs.astype(bf16)
        att_ref[rows, :] = dot(probs_low, values[seen, :]).astype(bf16)
        grad_probs = dot(grad_att[rows, :], values[seen, :], 1, 1)
        row_terms = jnp.sum(probs * grad_probs, axis=-1, keepdims=True)
        grad_scores = (probs * (grad_probs - row_terms)).astype(bf16)
        grad_queries = dot(grad_scores, keys[seen, :]) * factor
        grad_ref[rows, :head] = turn(grad_queries, tables(rows), -1.0).astype(bf16)
        grad_keys[seen, :] += dot(grad_scores, queries[rows, :], 0, 0)
        grad_values[seen, :] += dot(probs_low, grad_att[rows, :], 0, 0)
    for k in range(length // part):
        rows = slice(k * part, (k + 1) * part)
        grad_ref[rows, head : 2 * head] = turn(
            grad_keys[rows, :] * factor, tables(rows), -1.0
        ).astype(bf16)
        grad_ref[rows, 2 * head :] = grad_values[rows, :].astype(bf16)
        bias_ref[0:1, :] += jnp.sum(grad_ref[rows, :].astype(f32), axis=0, keepdims=True)
    cut = 512
    for k in range(width // cut):
        columns = slice(k * cut, (k + 1) * cut)
        qkv_total[:, columns] += dot(grad_ref[...], normed[:, columns], 0, 0)
        dense_total[:, columns] += dot(att_ref[...], up[:, columns], 0, 0)

    @pl.when(step == pl.num_programs(0) - 1)
    def _():
        dense_ref[...] = dense_total[...].astype(bf16)
        pack(sums_ref, qkv_total, 0, count)


def one_head(normed, up, w_qkv, b_qkv, w_dense, tables, seg_row, seg_col, length, count):
    rows, width = normed.shape
    head = w_dense.shape[0]
    lanes = tables[0].shape[1]
    wide = pl.BlockSpec((length, width), lambda i: (i, 0))
    thin = lambda columns: pl.BlockSpec((length, columns), lambda i: (i, 0))
    whole = lambda shape: pl.BlockSpec(shape, lambda i: (0,) * len(shape))
    sums = (count, 3 * head // count, width)
    return call(
        heads_kernel,
        20 * rows * width * head,
        4 * rows * width + 16 * width * head,
        grid=(rows // length,),
        in_specs=[
            wide, wide, whole(w_qkv.shape), whole(b_qkv.shape), whole(w_dense.shape),
            thin(lanes), thin(lanes), thin(lanes),
            pl.BlockSpec((None, 1, length), lambda i: (i, 0, 0)), thin(1),
        ],
        out_specs=[
            thin(head), thin(3 * head), whole((head, width)), whole(sums), whole((8, 3 * head))
        ],
        out_shape=[
            jax.ShapeDtypeStruct((rows, head), bf16),
            jax.ShapeDtypeStruct((rows, 3 * head), bf16),
            jax.ShapeDtypeStruct((head, width), bf16),
            jax.ShapeDtypeStruct(sums, bf16),
            jax.ShapeDtypeStruct((8, 3 * head), f32),
        ],
        scratch_shapes=[pltpu.VMEM((length, head), bf16)] * 4
        + [pltpu.VMEM((length, head), f32)] * 2
        + [pltpu.VMEM((3 * head, width), f32), pltpu.VMEM((head, width), f32)],
        name="one_head",
    )(normed, up, w_qkv, b_qkv, w_dense, *tables, seg_row, seg_col)


def out_kernel(core_ref, att, act, w_dense, w_down, out_ref):
    total = dot(att[...], w_dense[...])
    total += dot(act[...], w_down[...])
    out_ref[...] = total.astype(bf16)


def out_terms(core, att, act, w_dense, w_down, rows):
    width = w_dense.shape[1]
    tile = lambda array: pl.BlockSpec((rows, array.shape[1]), lambda i, c: (2 * i + c[0], 0))
    whole = lambda array: pl.BlockSpec(array.shape, lambda i, c: (0, 0))
    inner = w_dense.shape[0] + w_down.shape[0]
    return call(
        out_kernel,
        8 * rows * inner * width,
        2 * inner * width + 8 * rows * (inner + width),
        grid_spec=pltpu.PrefetchScalarGridSpec(
            num_scalar_prefetch=1,
            grid=(4,),
            in_specs=[tile(a) for a in (att, act)] + [whole(w) for w in (w_dense, w_down)],
            out_specs=pl.BlockSpec((None, rows, width), lambda i, c: (i, 0, 0)),
        ),
        out_shape=jax.ShapeDtypeStruct((4, rows, width), bf16),
        name="out_terms",
    )(core.reshape(1), att, act, w_dense, w_down)


def back_kernel(
    core_ref, tokens, mean, inv_std, params, grad_qkv, grad_hidden,
    w_qkv, w_up, out_ref, sums_ref,
):
    width = tokens.shape[1]

    @pl.when(pl.program_id(0) == 0)
    def _():
        sums_ref[...] = jnp.zeros_like(sums_ref)

    cut = 512
    for k in range(width // cut):
        columns = slice(k * cut, (k + 1) * cut)
        one = dot(grad_qkv[...], w_qkv[columns, :], 1, 1)
        two = dot(grad_hidden[...], w_up[columns, :], 1, 1)
        normed = (tokens[:, columns].astype(f32) - mean[...]) * inv_std[...]
        sums_ref[0:1, columns] += jnp.sum(one * normed, axis=0, keepdims=True)
        sums_ref[1:2, columns] += jnp.sum(one, axis=0, keepdims=True)
        sums_ref[2:3, columns] += jnp.sum(two * normed, axis=0, keepdims=True)
        sums_ref[3:4, columns] += jnp.sum(two, axis=0, keepdims=True)
        out_ref[:, columns] = (one * params[0:1, columns] + two * params[2:3, columns]).astype(
            bf16
        )


def back_terms(core, tokens, stats, params, grad_qkv, grad_hidden, w_qkv, w_up, rows):
    width = tokens.shape[1]
    tile = lambda array: pl.BlockSpec((rows, array.shape[1]), lambda i, c: (2 * i + c[0], 0))
    whole = lambda array: pl.BlockSpec(array.shape, lambda i, c: (0, 0))
    inner = w_qkv.shape[1] + w_up.shape[1]
    ins = [(tile, a) for a in (tokens, *stats)] + [(whole, params)]
    ins += [(tile, a) for a in (grad_qkv, grad_hidden)] + [(whole, a) for a in (w_qkv, w_up)]
    return call(
        back_kernel,
        8 * rows * inner * width,
        2 * inner * width + 8 * rows * (inner + 2 * width),
        grid_spec=pltpu.PrefetchScalarGridSpec(
            num_scalar_prefetch=1,
            grid=(4,),
            in_specs=[spec(array) for spec, array in ins],
            out_specs=[
                pl.BlockSpec((None, rows, width), lambda i, c: (i, 0, 0)),
                pl.BlockSpec((8, width), lambda i, c: (0, 0)),
            ],
        ),
        out_shape=[
            jax.ShapeDtypeStruct((4, rows, width), bf16),
            jax.ShapeDtypeStruct((8, width), f32),
        ],
        name="back_terms",
    )(core.reshape(1), *(array for _, array in ins))


class Block:
    def __init__(self):
        self.blocks = lax.axis_size("r")
        self.total = self.blocks * 8
        self.r = lax.axis_index("r")
        self.g = lax.axis_index("p") * 4 + lax.axis_index("seq")
        self.pq = self.g // 2
        self.deal = self.blocks == 4 and lax.axis_size("seq") == 4
        self.heads = [2 * (g % 4) + g // 4 if self.deal else g for g in range(8)]
        self.c = self.g % 2

    def swap(self, array, mask):
        return lax.ppermute(array, AXES, [(i, i ^ mask) for i in range(self.total)])

    def along(self, array, step, low, high):
        pairs = [
            (8 * r + g, 8 * ((r + step) % self.blocks) + g)
            for r in range(low, high)
            for g in range(8)
        ]
        return lax.ppermute(array, AXES, pairs)

    def gather_blocks(self, array, behind=()):
        return lax.all_gather(after(array, behind), "r")

    def scatter_blocks(self, parts):
        flat = parts.reshape((-1,) + parts.shape[2:])
        flat = with_layout_constraint(flat, Layout((0, 1)))
        return lax.psum_scatter(flat, "r", scatter_dimension=0, tiled=True)

    def line_small(self, array):
        count = self.blocks
        out = put(jnp.zeros((count,) + array.shape, array.dtype), array, self.r)
        for step in range(1, count):
            out = put(out, self.along(array, step, 0, count), (self.r - step) % count)
        return out

    def to_heads(self, array, back=False):
        count = self.blocks
        pairs = [(h * count + r, r * 8 + g) for g, h in enumerate(self.heads) for r in range(count)]
        if back:
            pairs = [(b, a) for a, b in pairs]
        return lax.ppermute(array, AXES, pairs)


class Split:
    def __init__(self, block, kept, sent):
        self.block = block
        half = kept.shape[1] // 2
        p, q = block.pq // 2, block.pq % 2

        def terms(at, rows):
            return pick(kept, at)[rows].astype(f32) + pick(sent, at)[rows].astype(f32)

        one, two = slice(0, half), slice(half, None)
        self.one_out = jnp.stack([terms((1 - p) * 2 + k, one).astype(bf16) for k in (0, 1)])
        self.two_out = jnp.stack([terms(k * 2 + 1 - q, two).astype(bf16) for k in (0, 1)])
        self.one = [terms(p * 2 + 1 - q, one), terms(p * 2 + q, one)]
        self.two = [terms((1 - p) * 2 + q, two), terms(p * 2 + q, two)]

    def round_one(self):
        self.one_in = self.block.swap(self.one_out, 4)
        self.two_in = self.block.swap(self.two_out, 2)

    def prepare(self):
        p, q = self.block.pq // 2, self.block.pq % 2
        self.one_out = (self.one[0] + pick(self.one_in, 1 - q).astype(f32)).astype(bf16)
        self.two_out = (self.two[0] + pick(self.two_in, 1 - p).astype(f32)).astype(bf16)
        self.one = self.one[1] + pick(self.one_in, q).astype(f32)
        self.two = self.two[1] + pick(self.two_in, p).astype(f32)

    def round_two(self):
        self.one_in = self.block.swap(self.one_out, 2)
        self.two_in = self.block.swap(self.two_out, 4)

    def finish(self):
        return jnp.concatenate(
            [self.one + self.one_in.astype(f32), self.two + self.two_in.astype(f32)]
        )


class Sums:
    def __init__(self, block, block_parts, own_parts):
        self.block, self.own_parts = block, own_parts
        parts = block_parts.reshape(block.blocks, 2, 2, 2, -1)
        self.parts = parts.transpose(3, 1, 2, 0, 4)

    def round(self, mask):
        block = self.block
        bit = {4: block.pq // 2, 2: block.pq % 2, 1: block.c}[mask]
        self.parts = pick(self.parts, bit) + block.swap(pick(self.parts, 1 - bit), mask)

    def finish(self):
        block, count = self.block, self.block.blocks
        parts = jnp.concatenate([self.parts, self.own_parts], axis=-1)
        total = pick(parts, block.r)
        for step in range(1, count):
            sent = block.along(pick(parts, (block.r + step) % count), step, 0, count)
            total = total + sent
        return total


class Rows:
    def __init__(self, block, array):
        self.block, self.mine = block, [array]

    def round_one(self):
        self.mine += [self.block.swap(self.mine[0], 2 * mask) for mask in (1, 2, 3)]

    def finish(self, cuts):
        block = self.block
        others = [block.swap(piece, 1) for piece in self.mine]
        index = [(block.pq ^ mask) * 2 + block.c for mask in range(4)]
        index += [(block.pq ^ mask) * 2 + 1 - block.c for mask in range(4)]
        return place(self.mine + others, index, cuts)


def phase(*movers):
    held = [
        {k: v for k, v in vars(m).items() if k not in ("block", "short", "shapes")}
        if not isinstance(m, (jax.Array, list, tuple)) else m
        for m in movers
    ]
    held = lax.optimization_barrier(held)
    for mover, values in zip(movers, held):
        if not isinstance(mover, (jax.Array, list, tuple)):
            vars(mover).update(values)
    return [h for m, h in zip(movers, held) if isinstance(m, (jax.Array, list, tuple))]


def rotary_tables(positions, lanes):
    half = ROT_DIMS // 2
    inverse = 10000.0 ** (-(2.0 * jnp.arange(half, dtype=f32)) / ROT_DIMS)
    angles = positions[..., None] * inverse
    cosines, sines = jnp.cos(angles), jnp.sin(angles)
    zeros = jnp.zeros_like(sines)
    rest = positions.shape + (lanes - ROT_DIMS,)
    return [
        jnp.concatenate([cosines, cosines, jnp.ones(rest, f32)], axis=-1),
        jnp.concatenate([-sines, zeros, jnp.zeros(rest, f32)], axis=-1),
        jnp.concatenate([zeros, sines, jnp.zeros(rest, f32)], axis=-1),
    ]


def on_device(
    tokens,
    segments,
    positions,
    ln1_gain,
    ln1_bias,
    ln2_gain,
    ln2_bias,
    qkv_weight,
    qkv_bias,
    dense_weight,
    dense_bias,
    fc1_weight,
    fc1_bias,
    fc2_weight,
    fc2_bias,
    cotangent,
):
    block = Block()
    count, total = block.blocks, block.total
    num_seqs, pos_dev, width = tokens.shape
    seq_len = segments.shape[1]
    rows = num_seqs * pos_dev
    group_rows = 8 * rows
    head_dim = width // HEADS
    near = qkv_weight.shape[0]
    units = fc2_weight.shape[0]
    half = units // 2
    own_tokens = tokens.reshape(rows, width)
    own_up = cotangent.reshape(rows, width)

    group = ("p", "seq")
    pieces = [fc2_weight] + ([dense_weight] if block.deal else [])
    row_parts = block.gather_blocks(jnp.concatenate(pieces))
    heads = jnp.stack([qkv_weight[:, 3 * head_dim * h : 3 * head_dim * (h + 1)] for h in block.heads])
    cols = jnp.swapaxes(fc1_weight.reshape(near, count, 8, units), 1, 2).reshape(near, 8, -1)
    cols = jnp.concatenate([jnp.swapaxes(cols, 0, 1), heads], axis=2)
    cols = lax.all_to_all(cols, group, 0, 0, tiled=True).reshape(8 * near, -1)
    cut = count * units
    w_up = block.gather_blocks(cols[:, :cut])
    vectors = [ln1_gain, ln1_bias, ln2_gain, ln2_bias, dense_bias, fc2_bias, qkv_bias, fc1_bias]
    small = jnp.concatenate([v.reshape(-1, near) for v in vectors])
    kinds = small.shape[0]
    places = jnp.concatenate([positions, segments]).astype(f32)[None]
    cols, small, places, up = phase(cols, small.astype(f32), places, own_up)

    upstream = Rows(block, up)
    upstream.round_one()
    far = block.swap(places, 4)
    far, small = phase(far, small)
    small = block.line_small(small)
    small_rows = jnp.zeros((16 * width,), bf16).at[: small.size].set(small.reshape(-1).astype(bf16))
    tokens_block = Rows(block, jnp.concatenate([own_tokens, small_rows.reshape(16, width)]))
    phase(upstream, tokens_block)
    tokens_block.round_one()
    first = block.pq // 2 == 0
    places = jnp.concatenate([jnp.where(first, places, far), jnp.where(first, far, places)])
    tables = [t.reshape(group_rows, -1) for t in rotary_tables(places[:, 0], 128)]
    seg_row = places[:, 1:]
    seg_col = places[:, 1].reshape(group_rows, 1)
    upstream, = upstream.finish([(0, rows)])
    upstream = upstream.reshape(group_rows, width)
    tables, seg_row, seg_col, upstream, row_parts = phase(
        tokens_block, tables, seg_row, seg_col, upstream, row_parts
    )
    if block.deal:
        w_dense = lax.all_to_all(row_parts[:, units:], "seq", 0, 0, tiled=True)
    else:
        w_dense = block.gather_blocks(block.to_heads(dense_weight))
    w_dense, w_down = w_dense.reshape(-1, width), row_parts[:, :units].reshape(-1, width)
    all_tokens, small = tokens_block.finish([(0, rows), (rows, 16)])
    all_tokens = all_tokens.reshape(group_rows, width)
    small = small.reshape(8, -1)[:, : total * kinds * near // 8].reshape(8, count, kinds, near)
    small = jnp.swapaxes(small, 0, 1).reshape(total, kinds, near).astype(f32)
    params = jnp.swapaxes(small[:, :6], 0, 1).reshape(6, width)
    out_bias = params[4] + params[5]
    params = jnp.concatenate([params, jnp.zeros((2, width), f32)])
    b_qkv = small[:, 6:9].reshape(8, 1, 3 * head_dim)
    b_qkv = pick(jnp.stack([b_qkv[h] for h in block.heads]), block.g)
    b_up = lax.dynamic_index_in_dim(
        small[:, 9:].reshape(count, 8, units), block.g, 1, keepdims=False
    ).reshape(1, -1)
    normed_one, normed_two, *stats = norms(all_tokens, params)
    normed_one, normed_two, stats, w_up, w_down, w_dense = phase(
        normed_one, normed_two, stats, w_up, w_down, w_dense
    )
    w_up = w_up.reshape(width, -1)
    w_qkv = block.gather_blocks(cols[:, cut:], w_up[:16]).reshape(width, -1)

    activated, grad_hidden, down_parts, up_parts, up_bias = hidden_units(
        normed_two, upstream, w_up, w_down, b_up, count
    )
    up_sum = block.scatter_blocks(up_parts)
    normed_one, activated, w_qkv = phase(normed_one, activated, w_qkv)

    attended, grad_projected, dense_part, parts, bias = one_head(
        normed_one, upstream, w_qkv, b_qkv, w_dense, tables, seg_row, seg_col, seq_len, count
    )
    own_sums = jnp.concatenate([b[0].reshape(count, -1) for b in (up_bias, bias)], axis=1)
    dense_part = dense_part.reshape(count, near, width)
    if block.deal:
        dense_part = lax.all_to_all(dense_part, "seq", 0, 0, tiled=True)
    parts = jnp.concatenate([dense_part, parts], axis=1)
    heads_sum = block.scatter_blocks(parts)
    attended, grad_projected, own_sums = phase(attended, grad_projected, own_sums)
    down_parts, _ = phase(down_parts, parts)
    down_sum = block.scatter_blocks(down_parts.reshape(count, units, width))

    core = block.c.astype(jnp.int32)
    back = functools.partial(
        back_terms, tokens=all_tokens, stats=stats, params=params, grad_qkv=grad_projected,
        grad_hidden=grad_hidden, w_qkv=w_qkv, w_up=w_up, rows=rows,
    )
    sent, sums_sent = back(1 - core)
    sent = block.swap(sent, 1)
    kept, sums_kept = back(core)
    sums = jnp.concatenate(
        [(sums_sent + sums_kept)[:4], jnp.sum(own_up.astype(f32), axis=0, keepdims=True)]
    )
    sums = jnp.swapaxes(sums.reshape(5, total, near), 0, 1).reshape(total, -1)
    sums = Sums(block, sums, own_sums)
    grad_normed = Split(block, kept, sent)
    up_sum, = phase(grad_normed, sums, up_sum)
    parts = up_sum.reshape(units, count, 8, near).transpose(2, 3, 1, 0)
    attended, parts = phase(grad_normed, sums, attended, parts)

    grad_normed.round_one()
    sums.round(1)
    sent = out_terms(1 - core, attended, activated, w_dense, w_down, rows)
    kept = out_terms(core, attended, activated, w_dense, w_down, rows)
    sent, kept, parts = phase(grad_normed, sums, sent, kept, parts)
    grad_normed.prepare()
    phase(grad_normed)

    grad_normed.round_two()
    sent = block.swap(sent, 1)
    sums.round(4)
    parts = lax.all_to_all(parts, group, 0, 0, tiled=True)
    out_sum = Split(block, kept, sent)
    phase(grad_normed, sums, out_sum)

    out_sum.round_one()
    sums.round(2)
    grad_normed = grad_normed.finish()
    grad_fc1_weight = parts.transpose(1, 2, 0, 3).reshape(near, -1).astype(f32)
    grad_normed, grad_fc1_weight, heads_sum = phase(
        out_sum, sums, grad_normed, grad_fc1_weight, heads_sum
    )
    out_sum.prepare()
    part = heads_sum[near:].reshape(-1, count, 8, near).transpose(2, 3, 1, 0)
    part, = phase(out_sum, part)

    out_sum.round_two()
    part = lax.all_to_all(part.reshape(8, near, -1), group, 0, 0, tiled=True)
    sums = sums.finish()
    sums, part = phase(out_sum, sums, part)

    grad_qkv_bias = block.to_heads(sums[5 * near + units :], back=True)
    output = (own_tokens.astype(f32) + out_sum.finish() + out_bias).astype(bf16)
    part = part.reshape((2, 4) + part.shape[1:])
    part = part.transpose(2, 1, 0, 3) if block.deal else part.transpose(2, 0, 1, 3)
    grad_qkv_weight = part.reshape(near, -1).astype(f32)
    grad_dense_weight = heads_sum[:near]
    if not block.deal:
        grad_dense_weight = block.to_heads(grad_dense_weight, back=True)
    grad_dense_weight = grad_dense_weight.astype(f32)
    output, grad_qkv_bias, grad_qkv_weight, grad_dense_weight, down_sum = phase(
        output, grad_qkv_bias, grad_qkv_weight, grad_dense_weight, down_sum
    )
    grad_fc2_weight = down_sum.astype(f32)

    grad_normed = grad_normed.astype(f32)
    values = own_tokens.astype(f32)
    own_up_wide = own_up.astype(f32)
    centred = values - jnp.mean(values, axis=-1, keepdims=True)
    own_std = lax.rsqrt(jnp.mean(centred * centred, axis=-1, keepdims=True) + 1e-05)
    own_normed = centred * own_std
    grad_tokens = own_up_wide + own_std * (
        grad_normed
        - jnp.mean(grad_normed, axis=-1, keepdims=True)
        - own_normed * jnp.mean(grad_normed * own_normed, axis=-1, keepdims=True)
    )

    return (
        output.reshape(tokens.shape),
        grad_tokens.reshape(tokens.shape),
        sums[:near],
        sums[near : 2 * near],
        sums[2 * near : 3 * near],
        sums[3 * near : 4 * near],
        grad_qkv_weight,
        grad_qkv_bias,
        grad_dense_weight,
        sums[4 * near : 5 * near],
        grad_fc1_weight,
        sums[5 * near : 5 * near + units],
        grad_fc2_weight,
        sums[4 * near : 5 * near],
    )


def solution(mesh):
    blocks = mesh.shape["dp"] // 2
    mesh = jax.sharding.Mesh(mesh.devices.reshape(blocks, 2, -1), AXES)
    dp = ("r", "p")
    token, ids, vector, matrix = P(dp, "seq", None), P(dp, None), P(AXES), P(AXES, None)
    return jax.shard_map(
        on_device,
        mesh=mesh,
        in_specs=(
            token, ids, ids, vector, vector, vector, vector, matrix, vector, matrix, vector,
            matrix, vector, matrix, vector, token,
        ),
        out_specs=(
            token, token, vector, vector, vector, vector, matrix, vector, matrix, vector,
            matrix, vector, matrix, vector,
        ),
        check_vma=False,
    )
```

```python
import functools

import jax
import jax.numpy as jnp
from jax import lax
from jax.experimental import pallas as pl
from jax.experimental.layout import Layout, with_layout_constraint
from jax.experimental.pallas import tpu as pltpu
from jax.sharding import PartitionSpec as P

HEADS = 8
ROT_DIMS = 64
AXES = ("r", "p", "seq")
VMEM_LIMIT = 60 * 1024 * 1024

root_half = 0.7071067811865476
inv_root_tau = 0.3989422804014327
bf16 = jnp.bfloat16
f32 = jnp.float32


def after(value, behind):
    return lax.optimization_barrier((value, behind))[0]


def pick(array, index):
    return lax.dynamic_index_in_dim(array, index, 0, keepdims=False)


def put(array, value, index):
    return lax.dynamic_update_index_in_dim(array, value, index, 0)


def dot(left, right, left_dim=1, right_dim=0):
    return lax.dot_general(
        left, right, (((left_dim,), (right_dim,)), ((), ())), preferred_element_type=f32
    )


def call(kernel, flops, moved, **settings):
    return pl.pallas_call(
        kernel,
        compiler_params=pltpu.CompilerParams(vmem_limit_bytes=VMEM_LIMIT),
        cost_estimate=pl.CostEstimate(flops=flops, bytes_accessed=moved, transcendentals=0),
        **settings,
    )


def place_kernel(cuts, index_ref, *refs):
    pieces, outs, (held, sems_in, sems_out) = refs[:8], refs[8:-3], refs[-3:]
    fetch = [pltpu.make_async_copy(p, held.at[k], sems_in.at[k]) for k, p in enumerate(pieces)]
    store = [
        pltpu.make_async_copy(
            held.at[k, pl.ds(start, size)], out.at[index_ref[k]], sems_out.at[k, n]
        )
        for k in range(8)
        for n, (out, (start, size)) in enumerate(zip(outs, cuts))
    ]
    for copy in fetch:
        copy.start()
    for k, copy in enumerate(fetch):
        copy.wait()
        for n in range(len(cuts)):
            store[k * len(cuts) + n].start()
    for copy in store:
        copy.wait()


def place(pieces, index, cuts):
    shape, kind = pieces[0].shape, pieces[0].dtype
    return call(
        functools.partial(place_kernel, cuts),
        0,
        4 * len(pieces) * pieces[0].size,
        in_specs=[pl.BlockSpec(memory_space=pltpu.SMEM)] + [pl.BlockSpec(memory_space=pl.ANY)] * 8,
        out_specs=[pl.BlockSpec(memory_space=pl.ANY)] * len(cuts),
        out_shape=[jax.ShapeDtypeStruct((8, size) + shape[1:], kind) for _, size in cuts],
        scratch_shapes=[
            pltpu.VMEM((8,) + shape, kind),
            pltpu.SemaphoreType.DMA((8,)),
            pltpu.SemaphoreType.DMA((8, len(cuts))),
        ],
        name="place_pieces",
    )(jnp.stack(index).astype(jnp.int32), *pieces)


def norm_kernel(tokens, params, one, two, mean_ref, inv_ref):
    values = tokens[...].astype(f32)
    average = jnp.mean(values, axis=-1, keepdims=True)
    centred = values - average
    inv_std = lax.rsqrt(jnp.mean(centred * centred, axis=-1, keepdims=True) + 1e-05)
    normed = centred * inv_std
    one[...] = (normed * params[0:1] + params[1:2]).astype(bf16)
    two[...] = (normed * params[2:3] + params[3:4]).astype(bf16)
    mean_ref[...] = average
    inv_ref[...] = inv_std


def norms(tokens, params):
    rows, width = tokens.shape
    tile = 256
    wide = pl.BlockSpec((tile, width), lambda i: (i, 0))
    thin = pl.BlockSpec((tile, 1), lambda i: (i, 0))
    return call(
        norm_kernel,
        10 * rows * width,
        6 * rows * width,
        grid=(rows // tile,),
        in_specs=[wide, pl.BlockSpec(params.shape, lambda i: (0, 0))],
        out_specs=[wide, wide, thin, thin],
        out_shape=[
            jax.ShapeDtypeStruct((rows, width), bf16),
            jax.ShapeDtypeStruct((rows, width), bf16),
            jax.ShapeDtypeStruct((rows, 1), f32),
            jax.ShapeDtypeStruct((rows, 1), f32),
        ],
        name="norms",
    )(tokens, params)


def pack(out_ref, total_ref, start, count):
    rows, width = total_ref.shape
    high, wide = rows // count, width // count
    for block in range(count):
        for part in range(count):
            out_ref[block, start : start + high, part * wide : (part + 1) * wide] = total_ref[
                part * high : (part + 1) * high, block * wide : (block + 1) * wide
            ].astype(bf16)


def hidden_kernel(
    normed, up, w_up, w_down, b_up, act_ref, grad_ref, down_ref, up_ref, bias_ref, down_total, up_total
):
    step = pl.program_id(0)
    count = up_ref.shape[0]
    tile, width = normed.shape

    @pl.when(step == 0)
    def _():
        down_total[...] = jnp.zeros_like(down_total)
        up_total[...] = jnp.zeros_like(up_total)
        bias_ref[...] = jnp.zeros_like(bias_ref)

    part = 256
    for k in range(tile // part):
        rows = slice(k * part, (k + 1) * part)
        pre = dot(normed[rows, :], w_up[...]) + b_up[...]
        grad_act = dot(up[rows, :], w_down[...], 1, 1)
        cdf = 0.5 * (1.0 + lax.erf(pre * root_half))
        slope = cdf + pre * jnp.exp(-0.5 * pre * pre) * inv_root_tau
        act_ref[rows, :] = (pre * cdf).astype(bf16)
        grad = (grad_act * slope).astype(bf16)
        grad_ref[rows, :] = grad
        bias_ref[0:1, :] += jnp.sum(grad.astype(f32), axis=0, keepdims=True)
    cut = 512
    for k in range(width // cut):
        columns = slice(k * cut, (k + 1) * cut)
        down_total[:, columns] += dot(act_ref[...], up[:, columns], 0, 0)
        up_total[:, columns] += dot(grad_ref[...], normed[:, columns], 0, 0)

    @pl.when(step == pl.num_programs(0) - 1)
    def _():
        down_ref[...] = down_total[...].astype(bf16)
        pack(up_ref, up_total, 0, count)


def hidden_units(normed, up, w_up, w_down, b_up, count):
    rows, width = normed.shape
    units = w_up.shape[1]
    tile = 512
    wide = pl.BlockSpec((tile, width), lambda i: (i, 0))
    thin = pl.BlockSpec((tile, units), lambda i: (i, 0))
    whole = lambda shape: pl.BlockSpec(shape, lambda i: (0,) * len(shape))
    sums = (count, units // count, width)
    return call(
        hidden_kernel,
        8 * rows * width * units,
        4 * rows * width + 4 * rows * units + 8 * width * units,
        grid=(rows // tile,),
        in_specs=[wide, wide, whole(w_up.shape), whole(w_down.shape), whole((1, units))],
        out_specs=[thin, thin, whole((units, width)), whole(sums), whole((8, units))],
        out_shape=[
            jax.ShapeDtypeStruct((rows, units), bf16),
            jax.ShapeDtypeStruct((rows, units), bf16),
            jax.ShapeDtypeStruct((units, width), bf16),
            jax.ShapeDtypeStruct(sums, bf16),
            jax.ShapeDtypeStruct((8, units), f32),
        ],
        scratch_shapes=[pltpu.VMEM((units, width), f32), pltpu.VMEM((units, width), f32)],
        name="hidden_units",
    )(normed, up, w_up, w_down, b_up)


def turn(vectors, tables, sign):
    cosines, ahead, behind = tables
    lanes = cosines.shape[1]
    half = ROT_DIMS // 2
    first = vectors[:, :lanes]
    mixed = pltpu.roll(first, lanes - half, 1) * ahead + pltpu.roll(first, half, 1) * behind
    return jnp.concatenate([first * cosines + sign * mixed, vectors[:, lanes:]], axis=1)


def heads_kernel(
    normed, up, w_qkv, b_qkv, w_dense, cosines, ahead, behind, seg_row, seg_col,
    att_ref, grad_ref, dense_ref, sums_ref, bias_ref,
    queries, keys, values, grad_att, grad_keys, grad_values, qkv_total, dense_total,
):
    step = pl.program_id(0)
    count = sums_ref.shape[0]
    length, width = normed.shape
    head = att_ref.shape[1]
    factor = head ** (-0.5)
    part = 256

    @pl.when(step == 0)
    def _():
        qkv_total[...] = jnp.zeros_like(qkv_total)
        dense_total[...] = jnp.zeros_like(dense_total)
        bias_ref[...] = jnp.zeros_like(bias_ref)

    def tables(rows):
        return cosines[rows, :], ahead[rows, :], behind[rows, :]

    for k in range(length // part):
        rows = slice(k * part, (k + 1) * part)
        projected = dot(normed[rows, :], w_qkv[...]) + b_qkv[...]
        queries[rows, :] = turn(projected[:, :head], tables(rows), 1.0).astype(bf16)
        keys[rows, :] = turn(projected[:, head : 2 * head], tables(rows), 1.0).astype(bf16)
        values[rows, :] = projected[:, 2 * head :].astype(bf16)
        grad_att[rows, :] = dot(up[rows, :], w_dense[...], 1, 1).astype(bf16)

    grad_keys[...] = jnp.zeros_like(grad_keys)
    grad_values[...] = jnp.zeros_like(grad_values)
    for k in range(length // part):
        rows, seen = slice(k * part, (k + 1) * part), slice(0, (k + 1) * part)
        seen_len = (k + 1) * part
        place_q = k * part + lax.broadcasted_iota(jnp.int32, (part, seen_len), 0)
        place_k = lax.broadcasted_iota(jnp.int32, (part, seen_len), 1)
        allowed = (seg_col[rows, :] == seg_row[:, seen]) & (place_k <= place_q)
        scores = jnp.where(allowed, dot(queries[rows, :], keys[seen, :], 1, 1) * factor, -1e30)
        expo = jnp.exp(scores - jnp.max(scores, axis=-1, keepdims=True))
        probs = expo * (1.0 / jnp.sum(expo, axis=-1, keepdims=True))
        probs_low = probs.astype(bf16)
        att_ref[rows, :] = dot(probs_low, values[seen, :]).astype(bf16)
        grad_probs = dot(grad_att[rows, :], values[seen, :], 1, 1)
        row_terms = jnp.sum(probs * grad_probs, axis=-1, keepdims=True)
        grad_scores = (probs * (grad_probs - row_terms)).astype(bf16)
        grad_queries = dot(grad_scores, keys[seen, :]) * factor
        grad_ref[rows, :head] = turn(grad_queries, tables(rows), -1.0).astype(bf16)
        grad_keys[seen, :] += dot(grad_scores, queries[rows, :], 0, 0)
        grad_values[seen, :] += dot(probs_low, grad_att[rows, :], 0, 0)
    for k in range(length // part):
        rows = slice(k * part, (k + 1) * part)
        grad_ref[rows, head : 2 * head] = turn(
            grad_keys[rows, :] * factor, tables(rows), -1.0
        ).astype(bf16)
        grad_ref[rows, 2 * head :] = grad_values[rows, :].astype(bf16)
        bias_ref[0:1, :] += jnp.sum(grad_ref[rows, :].astype(f32), axis=0, keepdims=True)
    cut = 512
    for k in range(width // cut):
        columns = slice(k * cut, (k + 1) * cut)
        qkv_total[:, columns] += dot(grad_ref[...], normed[:, columns], 0, 0)
        dense_total[:, columns] += dot(att_ref[...], up[:, columns], 0, 0)

    @pl.when(step == pl.num_programs(0) - 1)
    def _():
        dense_ref[...] = dense_total[...].astype(bf16)
        pack(sums_ref, qkv_total, 0, count)


def one_head(normed, up, w_qkv, b_qkv, w_dense, tables, seg_row, seg_col, length, count):
    rows, width = normed.shape
    head = w_dense.shape[0]
    lanes = tables[0].shape[1]
    wide = pl.BlockSpec((length, width), lambda i: (i, 0))
    thin = lambda columns: pl.BlockSpec((length, columns), lambda i: (i, 0))
    whole = lambda shape: pl.BlockSpec(shape, lambda i: (0,) * len(shape))
    sums = (count, 3 * head // count, width)
    return call(
        heads_kernel,
        20 * rows * width * head,
        4 * rows * width + 16 * width * head,
        grid=(rows // length,),
        in_specs=[
            wide, wide, whole(w_qkv.shape), whole(b_qkv.shape), whole(w_dense.shape),
            thin(lanes), thin(lanes), thin(lanes),
            pl.BlockSpec((None, 1, length), lambda i: (i, 0, 0)), thin(1),
        ],
        out_specs=[
            thin(head), thin(3 * head), whole((head, width)), whole(sums), whole((8, 3 * head))
        ],
        out_shape=[
            jax.ShapeDtypeStruct((rows, head), bf16),
            jax.ShapeDtypeStruct((rows, 3 * head), bf16),
            jax.ShapeDtypeStruct((head, width), bf16),
            jax.ShapeDtypeStruct(sums, bf16),
            jax.ShapeDtypeStruct((8, 3 * head), f32),
        ],
        scratch_shapes=[pltpu.VMEM((length, head), bf16)] * 4
        + [pltpu.VMEM((length, head), f32)] * 2
        + [pltpu.VMEM((3 * head, width), f32), pltpu.VMEM((head, width), f32)],
        name="one_head",
    )(normed, up, w_qkv, b_qkv, w_dense, *tables, seg_row, seg_col)


def out_kernel(core_ref, att, act, w_dense, w_down, out_ref):
    total = dot(att[...], w_dense[...])
    total += dot(act[...], w_down[...])
    out_ref[...] = total.astype(bf16)


def out_terms(core, att, act, w_dense, w_down, rows):
    width = w_dense.shape[1]
    tile = lambda array: pl.BlockSpec((rows, array.shape[1]), lambda i, c: (2 * i + c[0], 0))
    whole = lambda array: pl.BlockSpec(array.shape, lambda i, c: (0, 0))
    inner = w_dense.shape[0] + w_down.shape[0]
    return call(
        out_kernel,
        8 * rows * inner * width,
        2 * inner * width + 8 * rows * (inner + width),
        grid_spec=pltpu.PrefetchScalarGridSpec(
            num_scalar_prefetch=1,
            grid=(4,),
            in_specs=[tile(a) for a in (att, act)] + [whole(w) for w in (w_dense, w_down)],
            out_specs=pl.BlockSpec((None, rows, width), lambda i, c: (i, 0, 0)),
        ),
        out_shape=jax.ShapeDtypeStruct((4, rows, width), bf16),
        name="out_terms",
    )(core.reshape(1), att, act, w_dense, w_down)


def back_kernel(
    core_ref, tokens, mean, inv_std, params, grad_qkv, grad_hidden,
    w_qkv, w_up, out_ref, sums_ref,
):
    width = tokens.shape[1]

    @pl.when(pl.program_id(0) == 0)
    def _():
        sums_ref[...] = jnp.zeros_like(sums_ref)

    cut = 512
    for k in range(width // cut):
        columns = slice(k * cut, (k + 1) * cut)
        one = dot(grad_qkv[...], w_qkv[columns, :], 1, 1)
        two = dot(grad_hidden[...], w_up[columns, :], 1, 1)
        normed = (tokens[:, columns].astype(f32) - mean[...]) * inv_std[...]
        sums_ref[0:1, columns] += jnp.sum(one * normed, axis=0, keepdims=True)
        sums_ref[1:2, columns] += jnp.sum(one, axis=0, keepdims=True)
        sums_ref[2:3, columns] += jnp.sum(two * normed, axis=0, keepdims=True)
        sums_ref[3:4, columns] += jnp.sum(two, axis=0, keepdims=True)
        out_ref[:, columns] = (one * params[0:1, columns] + two * params[2:3, columns]).astype(
            bf16
        )


def back_terms(core, tokens, stats, params, grad_qkv, grad_hidden, w_qkv, w_up, rows):
    width = tokens.shape[1]
    tile = lambda array: pl.BlockSpec((rows, array.shape[1]), lambda i, c: (2 * i + c[0], 0))
    whole = lambda array: pl.BlockSpec(array.shape, lambda i, c: (0, 0))
    inner = w_qkv.shape[1] + w_up.shape[1]
    ins = [(tile, a) for a in (tokens, *stats)] + [(whole, params)]
    ins += [(tile, a) for a in (grad_qkv, grad_hidden)] + [(whole, a) for a in (w_qkv, w_up)]
    return call(
        back_kernel,
        8 * rows * inner * width,
        2 * inner * width + 8 * rows * (inner + 2 * width),
        grid_spec=pltpu.PrefetchScalarGridSpec(
            num_scalar_prefetch=1,
            grid=(4,),
            in_specs=[spec(array) for spec, array in ins],
            out_specs=[
                pl.BlockSpec((None, rows, width), lambda i, c: (i, 0, 0)),
                pl.BlockSpec((8, width), lambda i, c: (0, 0)),
            ],
        ),
        out_shape=[
            jax.ShapeDtypeStruct((4, rows, width), bf16),
            jax.ShapeDtypeStruct((8, width), f32),
        ],
        name="back_terms",
    )(core.reshape(1), *(array for _, array in ins))


class Block:
    def __init__(self):
        self.blocks = lax.axis_size("r")
        self.total = self.blocks * 8
        self.r = lax.axis_index("r")
        self.g = lax.axis_index("p") * 4 + lax.axis_index("seq")
        self.pq = self.g // 2
        self.deal = self.blocks == 4 and lax.axis_size("seq") == 4
        self.heads = [2 * (g % 4) + g // 4 if self.deal else g for g in range(8)]
        self.c = self.g % 2

    def swap(self, array, mask):
        return lax.ppermute(array, AXES, [(i, i ^ mask) for i in range(self.total)])

    def along(self, array, step, low, high):
        pairs = [
            (8 * r + g, 8 * ((r + step) % self.blocks) + g)
            for r in range(low, high)
            for g in range(8)
        ]
        return lax.ppermute(array, AXES, pairs)

    def gather_blocks(self, array, behind=()):
        return lax.all_gather(after(array, behind), "r")

    def scatter_blocks(self, parts):
        flat = parts.reshape((-1,) + parts.shape[2:])
        flat = with_layout_constraint(flat, Layout((0, 1)))
        return lax.psum_scatter(flat, "r", scatter_dimension=0, tiled=True)

    def line_small(self, array):
        count = self.blocks
        out = put(jnp.zeros((count,) + array.shape, array.dtype), array, self.r)
        for step in range(1, count):
            out = put(out, self.along(array, step, 0, count), (self.r - step) % count)
        return out

    def to_heads(self, array, back=False):
        count = self.blocks
        pairs = [(h * count + r, r * 8 + g) for g, h in enumerate(self.heads) for r in range(count)]
        if back:
            pairs = [(b, a) for a, b in pairs]
        return lax.ppermute(array, AXES, pairs)


class Split:
    def __init__(self, block, kept, sent):
        self.block = block
        half = kept.shape[1] // 2
        p, q = block.pq // 2, block.pq % 2

        def terms(at, rows):
            return pick(kept, at)[rows].astype(f32) + pick(sent, at)[rows].astype(f32)

        one, two = slice(0, half), slice(half, None)
        self.one_out = jnp.stack([terms((1 - p) * 2 + k, one).astype(bf16) for k in (0, 1)])
        self.two_out = jnp.stack([terms(k * 2 + 1 - q, two).astype(bf16) for k in (0, 1)])
        self.one = [terms(p * 2 + 1 - q, one), terms(p * 2 + q, one)]
        self.two = [terms((1 - p) * 2 + q, two), terms(p * 2 + q, two)]

    def round_one(self):
        self.one_in = self.block.swap(self.one_out, 4)
        self.two_in = self.block.swap(self.two_out, 2)

    def prepare(self):
        p, q = self.block.pq // 2, self.block.pq % 2
        self.one_out = (self.one[0] + pick(self.one_in, 1 - q).astype(f32)).astype(bf16)
        self.two_out = (self.two[0] + pick(self.two_in, 1 - p).astype(f32)).astype(bf16)
        self.one = self.one[1] + pick(self.one_in, q).astype(f32)
        self.two = self.two[1] + pick(self.two_in, p).astype(f32)

    def round_two(self):
        self.one_in = self.block.swap(self.one_out, 2)
        self.two_in = self.block.swap(self.two_out, 4)

    def finish(self):
        return jnp.concatenate(
            [self.one + self.one_in.astype(f32), self.two + self.two_in.astype(f32)]
        )


class Sums:
    def __init__(self, block, block_parts, own_parts):
        self.block, self.own_parts = block, own_parts
        parts = block_parts.reshape(block.blocks, 2, 2, 2, -1)
        self.parts = parts.transpose(3, 1, 2, 0, 4)

    def round(self, mask):
        block = self.block
        bit = {4: block.pq // 2, 2: block.pq % 2, 1: block.c}[mask]
        self.parts = pick(self.parts, bit) + block.swap(pick(self.parts, 1 - bit), mask)

    def finish(self):
        block, count = self.block, self.block.blocks
        parts = jnp.concatenate([self.parts, self.own_parts], axis=-1)
        total = pick(parts, block.r)
        for step in range(1, count):
            sent = block.along(pick(parts, (block.r + step) % count), step, 0, count)
            total = total + sent
        return total


class Rows:
    def __init__(self, block, array):
        self.block, self.mine = block, [array]

    def round_one(self):
        self.mine += [self.block.swap(self.mine[0], 2 * mask) for mask in (1, 2, 3)]

    def finish(self, cuts):
        block = self.block
        others = [block.swap(piece, 1) for piece in self.mine]
        index = [(block.pq ^ mask) * 2 + block.c for mask in range(4)]
        index += [(block.pq ^ mask) * 2 + 1 - block.c for mask in range(4)]
        return place(self.mine + others, index, cuts)


def phase(*movers):
    held = [
        {k: v for k, v in vars(m).items() if k not in ("block", "short", "shapes")}
        if not isinstance(m, (jax.Array, list, tuple)) else m
        for m in movers
    ]
    held = lax.optimization_barrier(held)
    for mover, values in zip(movers, held):
        if not isinstance(mover, (jax.Array, list, tuple)):
            vars(mover).update(values)
    return [h for m, h in zip(movers, held) if isinstance(m, (jax.Array, list, tuple))]


def widen_kernel(array, out_ref):
    out_ref[...] = array[...].astype(f32)


def widen(array):
    rows, width = array.shape
    tile = rows // 2
    spec = pl.BlockSpec((tile, width), lambda i: (i, 0))
    return call(
        widen_kernel,
        rows * width,
        6 * rows * width,
        grid=(rows // tile,),
        in_specs=[spec],
        out_specs=spec,
        out_shape=jax.ShapeDtypeStruct((rows, width), f32),
        name="widen",
    )(array)


def rotary_tables(positions, lanes):
    half = ROT_DIMS // 2
    inverse = 10000.0 ** (-(2.0 * jnp.arange(half, dtype=f32)) / ROT_DIMS)
    angles = positions[..., None] * inverse
    cosines, sines = jnp.cos(angles), jnp.sin(angles)
    zeros = jnp.zeros_like(sines)
    rest = positions.shape + (lanes - ROT_DIMS,)
    return [
        jnp.concatenate([cosines, cosines, jnp.ones(rest, f32)], axis=-1),
        jnp.concatenate([-sines, zeros, jnp.zeros(rest, f32)], axis=-1),
        jnp.concatenate([zeros, sines, jnp.zeros(rest, f32)], axis=-1),
    ]


def on_device(
    tokens,
    segments,
    positions,
    ln1_gain,
    ln1_bias,
    ln2_gain,
    ln2_bias,
    qkv_weight,
    qkv_bias,
    dense_weight,
    dense_bias,
    fc1_weight,
    fc1_bias,
    fc2_weight,
    fc2_bias,
    cotangent,
):
    block = Block()
    count, total = block.blocks, block.total
    num_seqs, pos_dev, width = tokens.shape
    seq_len = segments.shape[1]
    rows = num_seqs * pos_dev
    group_rows = 8 * rows
    head_dim = width // HEADS
    near = qkv_weight.shape[0]
    units = fc2_weight.shape[0]
    half = units // 2
    own_tokens = tokens.reshape(rows, width)
    own_up = cotangent.reshape(rows, width)

    group = ("p", "seq")
    pieces = [fc2_weight] + ([dense_weight] if block.deal else [])
    row_parts = block.gather_blocks(jnp.concatenate(pieces))
    heads = jnp.stack([qkv_weight[:, 3 * head_dim * h : 3 * head_dim * (h + 1)] for h in block.heads])
    cols = jnp.swapaxes(fc1_weight.reshape(near, count, 8, units), 1, 2).reshape(near, 8, -1)
    cols = jnp.concatenate([jnp.swapaxes(cols, 0, 1), heads], axis=2)
    cols = lax.all_to_all(cols, group, 0, 0, tiled=True).reshape(8 * near, -1)
    cut = count * units
    w_up = block.gather_blocks(cols[:, :cut])
    vectors = [ln1_gain, ln1_bias, ln2_gain, ln2_bias, dense_bias, fc2_bias, qkv_bias, fc1_bias]
    small = jnp.concatenate([v.reshape(-1, near) for v in vectors])
    kinds = small.shape[0]
    places = jnp.concatenate([positions, segments]).astype(f32)[None]
    cols, small, places, up = phase(cols, small.astype(f32), places, own_up)

    upstream = Rows(block, up)
    upstream.round_one()
    far = block.swap(places, 4)
    far, small = phase(far, small)
    small = block.line_small(small)
    small_rows = jnp.zeros((16 * width,), bf16).at[: small.size].set(small.reshape(-1).astype(bf16))
    tokens_block = Rows(block, jnp.concatenate([own_tokens, small_rows.reshape(16, width)]))
    phase(upstream, tokens_block)
    tokens_block.round_one()
    first = block.pq // 2 == 0
    places = jnp.concatenate([jnp.where(first, places, far), jnp.where(first, far, places)])
    tables = [t.reshape(group_rows, -1) for t in rotary_tables(places[:, 0], 128)]
    seg_row = places[:, 1:]
    seg_col = places[:, 1].reshape(group_rows, 1)
    upstream, = upstream.finish([(0, rows)])
    upstream = upstream.reshape(group_rows, width)
    tables, seg_row, seg_col, upstream, row_parts = phase(
        tokens_block, tables, seg_row, seg_col, upstream, row_parts
    )
    if block.deal:
        w_dense = lax.all_to_all(row_parts[:, units:], "seq", 0, 0, tiled=True)
    else:
        w_dense = block.gather_blocks(block.to_heads(dense_weight))
    w_dense, w_down = w_dense.reshape(-1, width), row_parts[:, :units].reshape(-1, width)
    all_tokens, small = tokens_block.finish([(0, rows), (rows, 16)])
    all_tokens = all_tokens.reshape(group_rows, width)
    small = small.reshape(8, -1)[:, : total * kinds * near // 8].reshape(8, count, kinds, near)
    small = jnp.swapaxes(small, 0, 1).reshape(total, kinds, near).astype(f32)
    params = jnp.swapaxes(small[:, :6], 0, 1).reshape(6, width)
    out_bias = params[4] + params[5]
    params = jnp.concatenate([params, jnp.zeros((2, width), f32)])
    b_qkv = small[:, 6:9].reshape(8, 1, 3 * head_dim)
    b_qkv = pick(jnp.stack([b_qkv[h] for h in block.heads]), block.g)
    b_up = lax.dynamic_index_in_dim(
        small[:, 9:].reshape(count, 8, units), block.g, 1, keepdims=False
    ).reshape(1, -1)
    normed_one, normed_two, *stats = norms(all_tokens, params)
    normed_one, normed_two, stats, w_up, w_down, w_dense = phase(
        normed_one, normed_two, stats, w_up, w_down, w_dense
    )
    w_up = w_up.reshape(width, -1)
    w_qkv = block.gather_blocks(cols[:, cut:], w_up[:16]).reshape(width, -1)

    activated, grad_hidden, down_parts, up_parts, up_bias = hidden_units(
        normed_two, upstream, w_up, w_down, b_up, count
    )
    up_sum = block.scatter_blocks(up_parts)
    normed_one, activated, w_qkv = phase(normed_one, activated, w_qkv)

    attended, grad_projected, dense_part, parts, bias = one_head(
        normed_one, upstream, w_qkv, b_qkv, w_dense, tables, seg_row, seg_col, seq_len, count
    )
    own_sums = jnp.concatenate([b[0].reshape(count, -1) for b in (up_bias, bias)], axis=1)
    dense_part = dense_part.reshape(count, near, width)
    if block.deal:
        dense_part = lax.all_to_all(dense_part, "seq", 0, 0, tiled=True)
    parts = jnp.concatenate([dense_part, parts], axis=1)
    heads_sum = block.scatter_blocks(parts)
    attended, grad_projected, own_sums = phase(attended, grad_projected, own_sums)
    down_parts, _ = phase(down_parts, parts)
    down_sum = block.scatter_blocks(down_parts.reshape(count, units, width))

    core = block.c.astype(jnp.int32)
    back = functools.partial(
        back_terms, tokens=all_tokens, stats=stats, params=params, grad_qkv=grad_projected,
        grad_hidden=grad_hidden, w_qkv=w_qkv, w_up=w_up, rows=rows,
    )
    sent, sums_sent = back(1 - core)
    sent = block.swap(sent, 1)
    kept, sums_kept = back(core)
    sums = jnp.concatenate(
        [(sums_sent + sums_kept)[:4], jnp.sum(own_up.astype(f32), axis=0, keepdims=True)]
    )
    sums = jnp.swapaxes(sums.reshape(5, total, near), 0, 1).reshape(total, -1)
    sums = Sums(block, sums, own_sums)
    grad_normed = Split(block, kept, sent)
    up_sum, = phase(grad_normed, sums, up_sum)
    parts = up_sum.reshape(units, count, 8, near).transpose(2, 3, 1, 0)
    attended, parts = phase(grad_normed, sums, attended, parts)

    grad_normed.round_one()
    sums.round(1)
    sent = out_terms(1 - core, attended, activated, w_dense, w_down, rows)
    kept = out_terms(core, attended, activated, w_dense, w_down, rows)
    sent, kept, parts = phase(grad_normed, sums, sent, kept, parts)
    grad_normed.prepare()
    phase(grad_normed)

    grad_normed.round_two()
    sent = block.swap(sent, 1)
    sums.round(4)
    parts = lax.all_to_all(parts, group, 0, 0, tiled=True)
    out_sum = Split(block, kept, sent)
    phase(grad_normed, sums, out_sum)

    out_sum.round_one()
    sums.round(2)
    grad_normed = grad_normed.finish()
    grad_fc1_weight = parts.transpose(1, 2, 0, 3).reshape(near, -1).astype(f32)
    grad_normed, grad_fc1_weight, heads_sum = phase(
        out_sum, sums, grad_normed, grad_fc1_weight, heads_sum
    )
    out_sum.prepare()
    part = heads_sum[near:].reshape(-1, count, 8, near).transpose(2, 3, 1, 0)
    part, = phase(out_sum, part)

    out_sum.round_two()
    part = lax.all_to_all(part.reshape(8, near, -1), group, 0, 0, tiled=True)
    sums = sums.finish()
    sums, part = phase(out_sum, sums, part)

    grad_qkv_bias = block.to_heads(sums[5 * near + units :], back=True)
    output = (own_tokens.astype(f32) + out_sum.finish() + out_bias).astype(bf16)
    part = part.reshape((2, 4) + part.shape[1:])
    part = part.transpose(2, 1, 0, 3) if block.deal else part.transpose(2, 0, 1, 3)
    grad_qkv_weight = part.reshape(near, -1).astype(f32)
    grad_dense_weight = heads_sum[:near]
    if not block.deal:
        grad_dense_weight = block.to_heads(grad_dense_weight, back=True)
    grad_dense_weight = grad_dense_weight.astype(f32)
    output, grad_qkv_bias, grad_qkv_weight, grad_dense_weight, down_sum = phase(
        output, grad_qkv_bias, grad_qkv_weight, grad_dense_weight, down_sum
    )
    grad_fc2_weight = widen(down_sum)

    grad_normed = grad_normed.astype(f32)
    values = own_tokens.astype(f32)
    own_up_wide = own_up.astype(f32)
    centred = values - jnp.mean(values, axis=-1, keepdims=True)
    own_std = lax.rsqrt(jnp.mean(centred * centred, axis=-1, keepdims=True) + 1e-05)
    own_normed = centred * own_std
    grad_tokens = own_up_wide + own_std * (
        grad_normed
        - jnp.mean(grad_normed, axis=-1, keepdims=True)
        - own_normed * jnp.mean(grad_normed * own_normed, axis=-1, keepdims=True)
    )

    return (
        output.reshape(tokens.shape),
        grad_tokens.reshape(tokens.shape),
        sums[:near],
        sums[near : 2 * near],
        sums[2 * near : 3 * near],
        sums[3 * near : 4 * near],
        grad_qkv_weight,
        grad_qkv_bias,
        grad_dense_weight,
        sums[4 * near : 5 * near],
        grad_fc1_weight,
        sums[5 * near : 5 * near + units],
        grad_fc2_weight,
        sums[4 * near : 5 * near],
    )


def solution(mesh):
    blocks = mesh.shape["dp"] // 2
    mesh = jax.sharding.Mesh(mesh.devices.reshape(blocks, 2, -1), AXES)
    dp = ("r", "p")
    token, ids, vector, matrix = P(dp, "seq", None), P(dp, None), P(AXES), P(AXES, None)
    return jax.shard_map(
        on_device,
        mesh=mesh,
        in_specs=(
            token, ids, ids, vector, vector, vector, vector, matrix, vector, matrix, vector,
            matrix, vector, matrix, vector, token,
        ),
        out_specs=(
            token, token, vector, vector, vector, vector, matrix, vector, matrix, vector,
            matrix, vector, matrix, vector,
        ),
        check_vma=False,
    )
```
